128 devices in a mesh: row: 16 (over y_lo, z, core), col: 8 (over x, y_hi).
Axes of the slice: x: 4, y: 4 (y_hi: 2, y_lo: 2; y = y_hi * 2 + y_lo), z: 4, core: 2. Of those that a mesh axis runs over, the one named last changes fastest.
Arguments:
- out_cotangent: bfloat16 [2048, 8192], P('row', 'col'), may hold values from -1.25 to 1.25
- saved_input: bfloat16 [2048, 8192], P('row', 'col'), may hold values from -6 to 6
- scan_output: bfloat16 [2048, 16384], P('col', 'row'), may hold values from -6 to 6
- gate_input: bfloat16 [2048, 16384], P('col', 'row'), may hold values from -8 to 8
- branch_grad: bfloat16 [2048, 16384], P('col', 'row'), may hold values from -1.25 to 1.25
- out_weight: bfloat16 [16384, 8192], P('row', 'col'), may hold values from -0.046875 to 0.046875
- in_weight: bfloat16 [8192, 2, 16384], P('col', None, 'row'), may hold values from -0.0625 to 0.0625
Outputs:
- input_grad: bfloat16 [2048, 8192], P('row', 'col')
- scan_grad: bfloat16 [2048, 16384], P('col', 'row')
- in_weight_grad: float32 [8192, 2, 16384], P('col', None, 'row')
- out_weight_grad: float32 [16384, 8192], P('row', 'col')
The draws below stay inside these ranges and needn't reach their ends.
All inputs are finite; a program needn't handle non-finite values.
Results may differ from the reference program's by a relative error of at most 0.025.
Values may be sent and summed in bfloat16 or wider, within the bound.
A program may use at most 192 MiB of HBM per device.

```python
import jax
import jax.numpy as jnp
from jax import lax

D = 8192
E = 16384
TOKENS = 2048
N_ROW = 16
N_COL = 8


def raised(values, key, source, target, blocks, factor):
    owner, partner = [(jnp.arange(values.shape[position]) // (values.shape[position] // blocks)).reshape([-1 if axis == position else 1 for axis in range(values.ndim)]) for position in (source, target)]
    chosen = jax.random.permutation(key, blocks)[partner]
    strong = (owner == chosen) | (owner == (partner + blocks // 2) % blocks)
    return jnp.where(strong, factor * values, values)


def shard_levels(own_key, dims, split, smallest, top_value):
    loudness = 1.0
    for dim, shards_of in split:
        draws = jax.random.uniform(jax.random.fold_in(jax.random.fold_in(own_key, 6), dim), (shards_of,), jnp.float32, smallest / len(split), top_value / len(split))
        loudness = loudness * jnp.repeat(jnp.exp(draws), dims[dim] // shards_of).reshape((-1,) + (1,) * (len(dims) - 1 - dim))
    return loudness


def noise(own_key, extent, spread, reach, pieces=(), kind=jnp.bfloat16):
    entries = jax.random.normal(own_key, extent, jnp.float32) * spread
    if len(pieces) > 0:
        entries = shard_levels(own_key, extent, pieces, -0.22, 0.18) * entries
    return jnp.clip(entries, min=-reach, max=reach).astype(kind)


def noise_with(key, dims, spread, limit, shards, heavy, kind=jnp.bfloat16):
    values = spread * jax.random.normal(key, dims, jnp.float32)
    if shards:
        values = values * shard_levels(key, dims, shards, -0.22, 0.18)
    return jnp.clip(raised(values, jax.random.fold_in(key, 3), *heavy), -limit, limit).astype(kind)


def setup_inputs(seed: int = 0) -> dict:
    streams_of = jax.random.split(jax.random.key(seed), 8)
    out_cotangent = noise_with(streams_of[0], (TOKENS, D), (1.0 / TOKENS ** 0.25), 1.25, ((0, 16), (1, 8)), (1, 0, 16, 2.0))
    saved_input = noise(streams_of[1], (TOKENS, D), 1.0, 6.0, ((0, 16), (1, 8)))
    scan_output = noise(streams_of[2], (TOKENS, E), 1.0, 6.0, ((0, 8), (1, 16)))
    gate_input = noise(streams_of[3], (TOKENS, E), 1.5, 8.0, ((0, 8), (1, 16)))
    branch_grad = noise_with(streams_of[4], (TOKENS, E), (1.0 / TOKENS ** 0.25), 1.25, ((0, 8), (1, 16)), (1, 0, 16, 2.0))
    out_weight = noise(streams_of[5], (E, D), E ** -0.5, 0.046875, ((0, 16), (1, 8)))
    in_weight = noise(streams_of[6], (D, 2, E), D ** -0.5, 0.0625, ((0, 8), (2, 16)))
    return dict(out_cotangent=out_cotangent, saved_input=saved_input, scan_output=scan_output, gate_input=gate_input, branch_grad=branch_grad, out_weight=out_weight, in_weight=in_weight)


def reference(out_cotangent, saved_input, scan_output, gate_input, branch_grad, out_weight, in_weight):
    gate_value = gate_input.astype(jnp.float32)
    sigmoid_gate = jax.nn.sigmoid(gate_value)
    silu_gate = gate_value * sigmoid_gate
    scan_value = scan_output.astype(jnp.float32)
    gated = (scan_value * silu_gate).astype(jnp.bfloat16)
    width = D // N_COL
    gated_grad = jnp.zeros((TOKENS, E), jnp.float32)
    for block in range(N_COL):
        part_rows = out_cotangent[:, block * width:(block + 1) * width]
        part_weight = out_weight[:, block * width:(block + 1) * width]
        partial_sum = lax.dot_general(part_rows, part_weight, (((1,), (1,)), ((), ())), preferred_element_type=jnp.float32)
        gated_grad = gated_grad + partial_sum.astype(jnp.bfloat16).astype(jnp.float32)
    gate_grad = (gated_grad * scan_value * sigmoid_gate * (1.0 + gate_value * (1.0 - sigmoid_gate))).astype(jnp.bfloat16)
    scan_grad = (gated_grad * silu_gate).astype(jnp.bfloat16)
    branch_weight = in_weight[:, 0, :]
    gate_weight = in_weight[:, 1, :]
    channels = E // N_ROW
    input_sum = jnp.zeros((TOKENS, D), jnp.float32)
    for block in range(N_ROW):
        low = block * channels
        high = low + channels
        term = lax.dot_general(branch_grad[:, low:high], branch_weight[:, low:high], (((1,), (1,)), ((), ())), preferred_element_type=jnp.float32)
        term = term + lax.dot_general(gate_grad[:, low:high], gate_weight[:, low:high], (((1,), (1,)), ((), ())), preferred_element_type=jnp.float32)
        input_sum = input_sum + term.astype(jnp.bfloat16).astype(jnp.float32)
    input_grad = input_sum.astype(jnp.bfloat16)
    branch_part = lax.dot_general(saved_input, branch_grad, (((0,), (0,)), ((), ())), preferred_element_type=jnp.float32)
    gate_part = lax.dot_general(saved_input, gate_grad, (((0,), (0,)), ((), ())), preferred_element_type=jnp.float32)
    in_weight_grad = jnp.stack([branch_part, gate_part], axis=1)
    out_weight_grad = lax.dot_general(gated, out_cotangent, (((0,), (0,)), ((), ())), preferred_element_type=jnp.float32)
    return input_grad, scan_grad, in_weight_grad, out_weight_grad
```

```python
import jax
import jax.numpy as jnp
from jax import lax
from jax.experimental import pallas as pl
from jax.experimental.pallas import tpu as pltpu
from jax.sharding import PartitionSpec as P

MESH = pl.DeviceIdType.MESH
F32 = jnp.float32
BF16 = jnp.bfloat16
REMOTE = 64
LOCAL = 12
NT = (((1,), (1,)), ((), ()))
NN = (((1,), (0,)), ((), ()))
TN = (((0,), (0,)), ((), ()))


def dot(a, b, dims):
    return lax.dot_general(a, b, dims, preferred_element_type=F32)


def kernel(
    cot_in,
    saved_in,
    scan_in,
    gate_in,
    branch_in,
    ow_in,
    iw_in,
    ig_out,
    sg_out,
    iwg_out,
    owg_out,
    cot,
    saved,
    branch,
    gated,
    ggrad,
    ow,
    iw,
    iw_raw,
    part,
    part2,
    r_y0,
    r_half,
    r_q,
    r_x,
    r_y1,
    r2_core,
    r2_q,
    r2_x,
    r2_y,
    scan_v,
    gate_v,
    sg_v,
    ig_v,
    stage,
    owg_stage,
    ssem,
    rsem,
    lsem,
    osem,
):
    row, col = lax.axis_index("row"), lax.axis_index("col")
    yl, z, k = row // 8, (row // 2) % 4, row % 2
    x, h = col // 2, col % 2
    j = yl * 4 + z
    c = col

    def device(x=x, h=h, yl=yl, z=z, k=k):
        return ((yl * 4 + z) * 2 + k, x * 2 + h)

    xp, xm, x2 = (x + 1) % 4, (x + 3) % 4, (x + 2) % 4
    zp, zm, z2 = (z + 1) % 4, (z + 3) % 4, (z + 2) % 4
    ho, yo, ko = 1 - h, 1 - yl, 1 - k
    XP, XM, YH = device(x=xp), device(x=xm), device(h=ho)
    ZP, ZM, Z2, YL, CO = device(z=zp), device(z=zm), device(z=z2), device(yl=yo), device(k=ko)

    used = [0, 0]
    sent = []

    def send(src, dst, to):
        i = used[0]
        used[0] += 1
        copy = pltpu.make_async_remote_copy(
            src_ref=src, dst_ref=dst, send_sem=ssem.at[i], recv_sem=rsem.at[i], device_id=to, device_id_type=MESH
        )
        copy.start()
        sent.append(copy)
        return copy

    def local(src, dst):
        i = used[1]
        used[1] += 1
        copy = pltpu.make_async_copy(src, dst, lsem.at[i])
        copy.start()
        return copy

    l_cot = local(cot_in, cot.at[j, k])
    l_branch = local(branch_in, branch.at[c])
    l_scan = local(scan_in, scan_v)
    l_gate = local(gate_in, gate_v)
    l_saved = local(saved_in, saved.at[j, k])
    l_iw = local(iw_in, iw_raw)
    l_ow = local(ow_in, ow)

    barrier = pltpu.get_barrier_semaphore()
    for peer in (XP, XM, YH, ZP, ZM, Z2, YL, CO):
        pl.semaphore_signal(barrier, inc=1, device_id=peer, device_id_type=MESH)
    pl.semaphore_wait(barrier, 8)

    def row_first(buf):
        own = buf.at[j, k]
        return [send(own, own, to) for to in (YL, ZP, ZM, Z2)]

    def row_second(buf, first):
        first[0].wait_recv()
        other = buf.at[yo * 4 + z, k]
        return [send(other, other, to) for to in (ZP, ZM, Z2)]

    def row_third(buf, first, second):
        for copy in first[1:] + second:
            copy.wait_recv()
        return send(buf.at[:, k], buf.at[:, k], CO)

    def col_first(buf):
        own = buf.at[c]
        return [send(own, own, to) for to in (YH, XP, XM)]

    def col_second(buf, first):
        first[1].wait_recv()
        top = buf.at[xm * 2 + h, pl.ds(0, 128)]
        a = send(top, top, XP)
        first[2].wait_recv()
        bottom = buf.at[xp * 2 + h, pl.ds(128, 128)]
        b = send(bottom, bottom, XM)
        first[0].wait_recv()
        other = buf.at[x * 2 + ho]
        return [a, b, send(other, other, XP), send(other, other, XM)]

    def col_third(buf, second):
        out = []
        for copy, half in ((second[0], 0), (second[1], 128)):
            copy.wait_recv()
            rows = buf.at[x2 * 2 + h, pl.ds(half, 128)]
            out.append(send(rows, rows, YH))
        return out

    l_cot.wait()
    cot_a = row_first(cot)
    l_branch.wait()
    branch_a = col_first(branch)

    l_scan.wait()
    l_gate.wait()

    def gate_rows(i, carry):
        rows = pl.ds(pl.multiple_of(i * 16, 16), 16)
        v = gate_v[rows].astype(F32)
        gated[c, rows] = (scan_v[rows].astype(F32) * (v * jax.nn.sigmoid(v))).astype(BF16)
        return carry

    lax.fori_loop(0, 16, gate_rows, 0)

    cot_b = row_second(cot, cot_a)

    l_iw.wait()
    to_row = lax.broadcasted_iota(jnp.int32, (256, 256), 0)
    from_row = lax.broadcasted_iota(jnp.int32, (256, 256), 1)
    permutation = ((to_row % 16) * 16 + to_row // 16 == from_row).astype(BF16)

    def take_apart(i, carry):
        raw = iw_raw[pl.ds(pl.multiple_of(i * 256, 256), 256)]
        apart = dot(permutation, raw, NN).astype(BF16)
        rows = pl.ds(pl.multiple_of(i * 16, 16), 16)
        for g in range(16):
            iw[g % 2, rows, (g // 2) * 128 : (g // 2 + 1) * 128] = apart[g * 16 : (g + 1) * 16]
        return carry

    lax.fori_loop(0, 64, take_apart, 0)

    cot_c = row_third(cot, cot_a, cot_b)
    branch_b = col_second(branch, branch_a)
    l_saved.wait()
    saved_a = row_first(saved)
    l_ow.wait()
    cot_c.wait_recv()

    def share(chunk):
        rows = cot[chunk].reshape(256, 1024)

        def columns(n, carry):
            at = pl.multiple_of(n * 256, 256)
            part[chunk, :, pl.ds(at, 256)] = dot(rows, ow[pl.ds(at, 256)], NT).astype(BF16)
            return carry

        lax.fori_loop(0, 4, columns, 0)

    def add_to(dst, *srcs):
        def rows_of(i, carry):
            rows = pl.ds(pl.multiple_of(i * 16, 16), 16)
            total = dst[rows].astype(F32)
            for src in srcs:
                total = total + src[rows].astype(F32)
            dst[rows] = total.astype(BF16)
            return carry

        lax.fori_loop(0, dst.shape[0] // 16, rows_of, 0)

    far_o, far, next_o, prev_o = x2 * 2 + ho, x2 * 2 + h, xp * 2 + ho, xm * 2 + ho
    nxt, prev, mine_o = xp * 2 + h, xm * 2 + h, x * 2 + ho
    share(far_o)
    d0 = send(part.at[far_o], r_y0, YH)
    share(next_o)
    q0 = send(part.at[next_o], r_q.at[0], XP)
    share(prev_o)
    q1 = send(part.at[prev_o], r_q.at[1], XM)
    share(far)
    share(nxt)
    e0 = send(part.at[nxt, pl.ds(128, 128)], r_x.at[0, pl.ds(128, 128)], XP)
    share(prev)
    e1 = send(part.at[prev, pl.ds(0, 128)], r_x.at[1, pl.ds(0, 128)], XM)
    share(mine_o)
    share(c)
    saved_b = row_second(saved, saved_a)
    d0.wait_recv()
    add_to(part.at[far], r_y0)
    f0 = send(part.at[far, pl.ds(0, 128)], r_half.at[0], XP)
    f1 = send(part.at[far, pl.ds(128, 128)], r_half.at[1], XM)
    q0.wait_recv()
    q1.wait_recv()
    add_to(part.at[mine_o], r_q.at[0], r_q.at[1])
    y1 = send(part.at[mine_o], r_y1, YH)
    branch_c = col_third(branch, branch_b)
    f0.wait_recv()
    add_to(part.at[nxt, pl.ds(0, 128)], r_half.at[0])
    g0 = send(part.at[nxt, pl.ds(0, 128)], r_x.at[0, pl.ds(0, 128)], XP)
    f1.wait_recv()
    add_to(part.at[prev, pl.ds(128, 128)], r_half.at[1])
    g1 = send(part.at[prev, pl.ds(128, 128)], r_x.at[1, pl.ds(128, 128)], XM)
    saved_c = row_third(saved, saved_a, saved_b)
    for copy in (e0, e1, y1, g0, g1):
        copy.wait_recv()

    def backward_rows(i, carry):
        rows = pl.ds(pl.multiple_of(i * 16, 16), 16)
        total = part[c, rows].astype(F32) + r_x[0, rows].astype(F32)
        total = total + r_x[1, rows].astype(F32) + r_y1[rows].astype(F32)
        v = gate_v[rows].astype(F32)
        s = jax.nn.sigmoid(v)
        ggrad[c, rows] = (total * scan_v[rows].astype(F32) * s * (1.0 + v * (1.0 - s))).astype(BF16)
        sg_v[rows] = (total * (v * s)).astype(BF16)
        return carry

    lax.fori_loop(0, 16, backward_rows, 0)
    ggrad_a = col_first(ggrad)
    l_sg = local(sg_v, sg_out)

    def input_share(chunk):
        def columns(n, carry):
            at = pl.multiple_of(n * 256, 256)
            total = dot(branch[chunk], iw[0, pl.ds(at, 256)], NT)
            total = total + dot(ggrad[chunk], iw[1, pl.ds(at, 256)], NT)
            part2[chunk, :, :, pl.ds(at, 256)] = total.astype(BF16).reshape(2, 128, 256)
            return carry

        lax.fori_loop(0, 4, columns, 0)

    for copy in branch_b[2:] + branch_c:
        copy.wait_recv()
    input_share(c)
    ggrad_b = col_second(ggrad, ggrad_a)
    gated_a = col_first(gated)
    for chunk in (prev, nxt, mine_o):
        input_share(chunk)
    ggrad_c = col_third(ggrad, ggrad_b)
    input_share(far)
    ggrad_b[2].wait_recv()
    input_share(prev_o)
    ggrad_b[3].wait_recv()
    input_share(next_o)
    gated_b = col_second(gated, gated_a)
    for copy in ggrad_c:
        copy.wait_recv()
    input_share(far_o)
    saved_c.wait_recv()
    core = send(part2.at[:, ko], r2_core, CO)

    def in_weight_rows(i):
        slot = i % 2
        out = pltpu.make_async_copy(
            stage.at[slot], iwg_out.at[pl.ds(pl.multiple_of(i * 4096, 4096), 4096)], osem.at[slot]
        )

        @pl.when(i >= 2)
        def _():
            out.wait()

        features = pl.ds(pl.multiple_of(i * 256, 256), 256)
        lhs = saved[:, :, :, features].reshape(2048, 256)
        for half, buf in ((0, branch), (1, ggrad)):
            for n in range(4):
                rhs = buf[:, :, n * 256 : (n + 1) * 256].reshape(2048, 256)
                res = dot(lhs, rhs, TN)
                for t in range(2):
                    stage[slot, pl.ds(2 * (2 * n + t) + half, 256, stride=16), :] = res[:, t * 128 : (t + 1) * 128]
        out.start()

    def out_weight_rows(i):
        out = pltpu.make_async_copy(
            owg_stage, owg_out.at[pl.ds(pl.multiple_of(i * 256, 256), 256)], osem.at[2]
        )

        @pl.when(i >= 1)
        def _():
            out.wait()

        lhs = gated[:, :, pl.ds(pl.multiple_of(i * 256, 256), 256)].reshape(2048, 256)
        for n in range(4):
            rhs = cot[:, :, :, n * 256 : (n + 1) * 256].reshape(2048, 256)
            owg_stage[:, n * 256 : (n + 1) * 256] = dot(lhs, rhs, TN)
        out.start()

    def loop(low, high, body):
        def step(i, carry):
            body(i)
            return carry

        lax.fori_loop(low, high, step, 0)

    loop(0, 2, in_weight_rows)
    core.wait_recv()
    def add_cores(i, carry):
        rows = pl.ds(pl.multiple_of((i % 4) * 32, 32), 32)
        total = part2[i // 4, k, rows].astype(F32) + r2_core[i // 4, rows].astype(F32)
        part2[i // 4, k, rows] = total.astype(BF16)
        return carry

    lax.fori_loop(0, 32, add_cores, 0)
    rs_q = [send(part2.at[yo * 4 + to, k], r2_q.at[i], dev) for i, (to, dev) in enumerate(((zp, ZP), (zm, ZM), (z2, Z2)))]
    rs_x = [send(part2.at[yl * 4 + to, k], r2_x.at[i], dev) for i, (to, dev) in enumerate(((zp, ZP), (zm, ZM), (z2, Z2)))]
    loop(2, 3, in_weight_rows)
    gated_c = col_third(gated, gated_b)
    for copy in rs_q:
        copy.wait_recv()
    add_to(part2.at[yo * 4 + z, k], r2_q.at[0], r2_q.at[1], r2_q.at[2])
    rs_y = send(part2.at[yo * 4 + z, k], r2_y, YL)
    loop(3, 4, in_weight_rows)
    for copy in rs_x + [rs_y]:
        copy.wait_recv()

    def last_rows(i, carry):
        rows = pl.ds(pl.multiple_of(i * 16, 16), 16)
        total = part2[j, k, rows].astype(F32) + r2_y[rows].astype(F32)
        for t in range(3):
            total = total + r2_x[t, rows].astype(F32)
        ig_v[rows] = total.astype(BF16)
        return carry

    lax.fori_loop(0, 8, last_rows, 0)
    l_ig = local(ig_v, ig_out)
    for copy in gated_b[2:] + gated_c:
        copy.wait_recv()
    loop(0, 4, out_weight_rows)
    for slot in range(2):
        pltpu.make_async_copy(stage.at[slot], iwg_out.at[pl.ds(0, 4096)], osem.at[slot]).wait()
    pltpu.make_async_copy(owg_stage, owg_out.at[pl.ds(0, 256)], osem.at[2]).wait()
    l_sg.wait()
    l_ig.wait()
    for copy in sent:
        copy.wait_send()


def per_device(cot, saved, scan, gate, branch, ow, iw):
    iw = iw.reshape(1024, 2, 8, 128).transpose(0, 2, 1, 3).reshape(16384, 128)
    anywhere = pl.BlockSpec(memory_space=pl.ANY)
    vmem = pltpu.VMEM
    ig, sg, iwg, owg = pl.pallas_call(
        kernel,
        out_shape=[
            jax.ShapeDtypeStruct((128, 1024), BF16),
            jax.ShapeDtypeStruct((256, 1024), BF16),
            jax.ShapeDtypeStruct((16384, 128), F32),
            jax.ShapeDtypeStruct((1024, 1024), F32),
        ],
        in_specs=[anywhere] * 7,
        out_specs=[anywhere] * 4,
        scratch_shapes=[
            vmem((8, 2, 128, 1024), BF16),
            vmem((8, 2, 128, 1024), BF16),
            vmem((8, 256, 1024), BF16),
            vmem((8, 256, 1024), BF16),
            vmem((8, 256, 1024), BF16),
            vmem((1024, 1024), BF16),
            vmem((2, 1024, 1024), BF16),
            vmem((16384, 128), BF16),
            vmem((8, 256, 1024), BF16),
            vmem((8, 2, 128, 1024), BF16),
            vmem((256, 1024), BF16),
            vmem((2, 128, 1024), BF16),
            vmem((2, 256, 1024), BF16),
            vmem((2, 256, 1024), BF16),
            vmem((256, 1024), BF16),
            vmem((8, 128, 1024), BF16),
            vmem((3, 128, 1024), BF16),
            vmem((3, 128, 1024), BF16),
            vmem((128, 1024), BF16),
            vmem((256, 1024), BF16),
            vmem((256, 1024), BF16),
            vmem((256, 1024), BF16),
            vmem((128, 1024), BF16),
            vmem((2, 4096, 128), F32),
            vmem((256, 1024), F32),
            pltpu.SemaphoreType.DMA((REMOTE,)),
            pltpu.SemaphoreType.DMA((REMOTE,)),
            pltpu.SemaphoreType.DMA((LOCAL,)),
            pltpu.SemaphoreType.DMA((3,)),
        ],
        compiler_params=pltpu.CompilerParams(
            collective_id=0, has_side_effects=True, vmem_limit_bytes=60 * 1024 * 1024
        ),
        name="mixer_backward",
    )(cot, saved, scan, gate, branch, ow, iw)
    iwg = iwg.reshape(1024, 8, 2, 128).transpose(0, 2, 1, 3).reshape(1024, 2, 1024)
    return ig, sg, iwg, owg


def solution(mesh):
    return jax.shard_map(
        per_device,
        mesh=mesh,
        in_specs=(
            P("row", "col"),
            P("row", "col"),
            P("col", "row"),
            P("col", "row"),
            P("col", "row"),
            P("row", "col"),
            P("col", None, "row"),
        ),
        out_specs=(P("row", "col"), P("col", "row"), P("col", None, "row"), P("row", "col")),
        check_vma=False,
    )
```

```python
import jax
import jax.numpy as jnp
from jax import lax
from jax.experimental import pallas as pl
from jax.experimental.pallas import tpu as pltpu
from jax.sharding import PartitionSpec as P

MESH = pl.DeviceIdType.MESH
F32 = jnp.float32
BF16 = jnp.bfloat16
REMOTE = 96
VMEM_LIMIT = 40 * 1024 * 1024
LOCAL = 24
NT = (((1,), (1,)), ((), ()))
NN = (((1,), (0,)), ((), ()))
TN = (((0,), (0,)), ((), ()))


def dot(a, b, dims):
    return lax.dot_general(a, b, dims, preferred_element_type=F32)


def loop(low, high, body):
    def step(i, carry):
        body(i)
        return carry

    lax.fori_loop(low, high, step, 0)


def tokens_of(buf, chunks, columns):
    return jnp.concatenate([buf[:, chunk, :, columns].reshape(256, 256) for chunk in chunks])


def out_weight_part(gated, cot, out, i, chunks, first):
    rows = pl.ds(i * 256, 256)
    lhs = tokens_of(gated, chunks, rows)

    def columns(n):
        at = pl.ds(pl.multiple_of(n * 256, 256), 256)
        res = dot(lhs, tokens_of(cot, chunks, at), TN)
        out[rows, at] = res if first else out[rows, at] + res

    loop(0, 4, columns)


def kernel(
    cot_in,
    saved_in,
    scan_in,
    gate_in,
    branch_in,
    ow_in,
    iw_in,
    ig_v,
    sg_v,
    iwg_v,
    owg_v,
    cot,
    gated,
    saved,
    branch,
    ggrad,
    ow,
    iw,
    iw_raw,
    part,
    part2,
    r_y0,
    r_half,
    r_q,
    r_x,
    r_y1,
    r2_core,
    r2_y0,
    r2_q,
    r2_x,
    r2_y,
    scan_v,
    gate_v,
    ssem,
    rsem,
    lsem,
):
    row, col = lax.axis_index("row"), lax.axis_index("col")
    yl, z, k = row // 8, (row // 2) % 4, row % 2
    x, h = col // 2, col % 2
    j = yl * 4 + z
    c = col

    def device(x=x, h=h, yl=yl, z=z, k=k):
        return ((yl * 4 + z) * 2 + k, x * 2 + h)

    xp, xm, x2 = (x + 1) % 4, (x + 3) % 4, (x + 2) % 4
    zp, zm, z2 = (z + 1) % 4, (z + 3) % 4, (z + 2) % 4
    ho, yo, ko = 1 - h, 1 - yl, 1 - k
    XP, XM, YH = device(x=xp), device(x=xm), device(h=ho)
    ZP, ZM, Z2, YL, CO = device(z=zp), device(z=zm), device(z=z2), device(yl=yo), device(k=ko)
    far_o, far, next_o, prev_o = x2 * 2 + ho, x2 * 2 + h, xp * 2 + ho, xm * 2 + ho
    nxt, prev, mine_o = xp * 2 + h, xm * 2 + h, x * 2 + ho

    used = [0, 0]
    sent = []

    def send(src, dst, to):
        i = used[0]
        used[0] += 1
        copy = pltpu.make_async_remote_copy(
            src_ref=src, dst_ref=dst, send_sem=ssem.at[i], recv_sem=rsem.at[i], device_id=to, device_id_type=MESH
        )
        copy.start()
        sent.append(copy)
        return copy

    def local(src, dst):
        i = used[1]
        used[1] += 1
        copy = pltpu.make_async_copy(src, dst, lsem.at[i])
        copy.start()
        return copy

    def arrived(*copies):
        for copy in copies:
            copy.wait_recv()

    def done(copies):
        for copy in copies:
            copy.wait()

    def row_block(src, buf):
        return [local(src.at[pl.ds(b * 64, 64)], buf.at[b, j, pl.ds(k * 64, 64)]) for b in range(2)]

    def col_block(src, dst):
        return [
            local(src.at[pl.ds(core * 128 + b * 64, 64)], dst(b).at[pl.ds(core * 64, 64)])
            for core in range(2)
            for b in range(2)
        ]

    l_cot = row_block(cot_in, cot)
    l_branch = col_block(branch_in, lambda b: branch.at[b, c])
    l_scan = col_block(scan_in, lambda b: scan_v.at[b])
    l_gate = col_block(gate_in, lambda b: gate_v.at[b])
    l_saved = row_block(saved_in, saved)
    l_iw = [local(iw_in.at[pl.ds(p * 4096, 4096)], iw_raw.at[p]) for p in range(2)]
    l_ow = [local(ow_in, ow)]

    barrier = pltpu.get_barrier_semaphore()
    for peer in (XP, XM, YH, ZP, ZM, Z2, YL, CO):
        pl.semaphore_signal(barrier, inc=1, device_id=peer, device_id_type=MESH)
    pl.semaphore_wait(barrier, 8)

    def mine_of(buf, chip, b):
        return buf.at[:, chip, pl.ds(k * 64, 64)] if b is None else buf.at[b, chip, pl.ds(k * 64, 64)]

    def row_first(buf, b=None):
        own = mine_of(buf, j, b)
        return [send(own, own, to) for to in (YL, Z2, ZP, ZM)]

    def row_second(buf, first, b=None):
        arrived(first[0])
        other = mine_of(buf, yo * 4 + z, b)
        return [send(other, other, to) for to in ((ZP, ZM, Z2) if b is None else (ZP, ZM))]

    def row_third(buf, first, b):
        arrived(first[1])
        far_z = mine_of(buf, yl * 4 + z2, b)
        return send(far_z, far_z, YL)

    def cores(buf, b):
        block = buf.at[b, :, pl.ds(k * 64, 64)]
        return send(block, block, CO)

    def col_first(at, to=(YH, XP, XM)):
        return [send(at(c), at(c), peer) for peer in to]

    def col_second(at, first):
        arrived(first[1])
        a = send(at(prev, 0), at(prev, 0), XP)
        arrived(first[2])
        b = send(at(nxt, 1), at(nxt, 1), XM)
        arrived(first[0])
        return [a, b, send(at(mine_o), at(mine_o), XP), send(at(mine_o), at(mine_o), XM)]

    def col_third(at, second):
        out = []
        for half in range(2):
            arrived(second[half])
            out.append(send(at(far, half), at(far, half), YH))
        return out

    def col_third_x(at, second):
        arrived(second[2])
        a = send(at(prev_o, 0), at(prev_o, 0), XP)
        arrived(second[3])
        return [a, send(at(next_o, 1), at(next_o, 1), XM)]

    def whole(buf):
        def at(chunk, half=None):
            return buf.at[:, chunk] if half is None else buf.at[half, chunk]

        return at

    def batch(buf, b):
        def at(chunk, half=None):
            return buf.at[b, chunk] if half is None else buf.at[b, chunk, pl.ds(half * 64, 64)]

        return at

    to_row = lax.broadcasted_iota(jnp.int32, (256, 256), 0)
    from_row = lax.broadcasted_iota(jnp.int32, (256, 256), 1)
    permutation = ((to_row % 16) * 16 + to_row // 16 == from_row).astype(BF16)

    def take_apart(p):
        slot = p % 2
        l_iw[p].wait()

        def block(i):
            raw = iw_raw[slot, pl.ds(pl.multiple_of(i * 256, 256), 256)]
            apart = dot(permutation, raw, NN).astype(BF16)
            rows = pl.ds(pl.multiple_of(p * 256 + i * 16, 16), 16)
            for g in range(16):
                iw[g % 2, rows, (g // 2) * 128 : (g // 2 + 1) * 128] = apart[g * 16 : (g + 1) * 16]

        loop(0, 16, block)
        if p < 2:
            l_iw.append(local(iw_in.at[pl.ds((p + 2) * 4096, 4096)], iw_raw.at[slot]))

    def add_to(dst, *srcs):
        def rows_of(i):
            rows = pl.ds(pl.multiple_of(i * 16, 16), 16)
            total = dst[rows].astype(F32)
            for src in srcs:
                total = total + src[rows].astype(F32)
            dst[rows] = total.astype(BF16)

        loop(0, dst.shape[0] // 16, rows_of)

    def gate_forward():
        def rows_of(i):
            b, rows = i // 8, pl.ds(pl.multiple_of((i % 8) * 16, 16), 16)
            v = gate_v[b, rows].astype(F32)
            gated[b, c, rows] = (scan_v[b, rows].astype(F32) * (v * jax.nn.sigmoid(v))).astype(BF16)

        loop(0, 16, rows_of)

    def share(b):
        rows = cot[b].reshape(1024, 1024)

        def columns(n):
            at = pl.ds(pl.multiple_of(n * 256, 256), 256)
            part[b, :, :, at] = dot(rows, ow[at], NT).astype(BF16).reshape(8, 128, 256)

        loop(0, 4, columns)

    LOW, HIGH = pl.ds(0, 64), pl.ds(64, 64)

    def sum0(b):
        return dict(
            d=send(part.at[b, far_o], r_y0.at[b], YH),
            q=[send(part.at[b, next_o], r_q.at[b, 0], XP), send(part.at[b, prev_o], r_q.at[b, 1], XM)],
            e=[
                send(part.at[b, nxt, HIGH], r_x.at[b, 0, HIGH], XP),
                send(part.at[b, prev, LOW], r_x.at[b, 1, LOW], XM),
            ],
        )

    def sum1(b, s):
        arrived(s["d"])
        add_to(part.at[b, far], r_y0.at[b])
        s["f"] = [
            send(part.at[b, far, LOW], r_half.at[b, 0], XP),
            send(part.at[b, far, HIGH], r_half.at[b, 1], XM),
        ]

    def sum2(b, s):
        arrived(*s["q"])
        add_to(part.at[b, mine_o], r_q.at[b, 0], r_q.at[b, 1])
        s["y"] = send(part.at[b, mine_o], r_y1.at[b], YH)

    def sum3(b, s):
        arrived(s["f"][0])
        add_to(part.at[b, nxt, LOW], r_half.at[b, 0])
        g0 = send(part.at[b, nxt, LOW], r_x.at[b, 0, LOW], XP)
        arrived(s["f"][1])
        add_to(part.at[b, prev, HIGH], r_half.at[b, 1])
        g1 = send(part.at[b, prev, HIGH], r_x.at[b, 1, HIGH], XM)
        s["g"] = [g0, g1]

    def sum4(b, s):
        arrived(*s["e"], s["y"], *s["g"])

        def rows_of(i):
            rows = pl.ds(pl.multiple_of(i * 16, 16), 16)
            total = part[b, c, rows].astype(F32) + r_x[b, 0, rows].astype(F32)
            total = total + r_x[b, 1, rows].astype(F32) + r_y1[b, rows].astype(F32)
            v = gate_v[b, rows].astype(F32)
            s = jax.nn.sigmoid(v)
            ggrad[b, c, rows] = (total * scan_v[b, rows].astype(F32) * s * (1.0 + v * (1.0 - s))).astype(BF16)
            sg_v[pl.ds(pl.multiple_of((i // 4) * 128 + b * 64 + (i % 4) * 16, 16), 16)] = (total * (v * s)).astype(BF16)

        loop(0, 8, rows_of)
        return col_first(batch(ggrad, b))

    def input_share(b):
        def columns(n):
            at = pl.ds(pl.multiple_of(n * 256, 256), 256)
            total = dot(branch[b].reshape(1024, 1024), iw[0, at], NT)
            total = total + dot(ggrad[b].reshape(1024, 1024), iw[1, at], NT)
            part2[b, :, :, at] = total.astype(BF16).reshape(8, 128, 256)

        loop(0, 4, columns)

    MINE = pl.ds(pl.multiple_of(k * 64, 64), 64)
    OTHER = pl.ds(pl.multiple_of(ko * 64, 64), 64)

    def row0(b):
        return dict(c=send(part2.at[b, :, OTHER], r2_core.at[b], CO))

    def row1(b, s):
        arrived(s["c"])

        def chip(i):
            total = part2[b, i, MINE].astype(F32) + r2_core[b, i].astype(F32)
            part2[b, i, MINE] = total.astype(BF16)

        loop(0, 8, chip)
        s["d"] = send(part2.at[b, yo * 4 + z2, MINE], r2_y0.at[b], YL)
        s["q"] = [
            send(part2.at[b, yo * 4 + zp, MINE], r2_q.at[b, 0], ZP),
            send(part2.at[b, yo * 4 + zm, MINE], r2_q.at[b, 1], ZM),
        ]

    def row2(b, s):
        arrived(s["d"])
        add_to(part2.at[b, yl * 4 + z2, MINE], r2_y0.at[b])
        s["x"] = [
            send(part2.at[b, yl * 4 + z2, MINE], r2_x.at[b, 2], Z2),
            send(part2.at[b, yl * 4 + zp, MINE], r2_x.at[b, 0], ZP),
            send(part2.at[b, yl * 4 + zm, MINE], r2_x.at[b, 1], ZM),
        ]

    def row3(b, s):
        arrived(*s["q"])
        add_to(part2.at[b, yo * 4 + z, MINE], r2_q.at[b, 0], r2_q.at[b, 1])
        s["y"] = send(part2.at[b, yo * 4 + z, MINE], r2_y.at[b], YL)

    def row4(b, s):
        arrived(*s["x"], s["y"])

        def rows_of(i):
            rows = pl.ds(pl.multiple_of(i * 16, 16), 16)
            own = pl.ds(pl.multiple_of(k * 64 + i * 16, 16), 16)
            total = part2[b, j, own].astype(F32) + r2_y[b, rows].astype(F32)
            for t in range(3):
                total = total + r2_x[b, t, rows].astype(F32)
            ig_v[pl.ds(pl.multiple_of(b * 64 + i * 16, 16), 16)] = total.astype(BF16)

        loop(0, 4, rows_of)

    def in_weight_rows(half, i):
        buf = (branch, ggrad)[half]
        lhs = saved[:, :, :, i * 256 : (i + 1) * 256].reshape(2048, 256)

        def columns(n):
            at = pl.ds(pl.multiple_of(n * 256, 256), 256)
            res = dot(lhs, buf[:, :, :, at].reshape(2048, 256), TN)
            for t in range(2):
                iwg_v[pl.ds(i * 4096 + 4 * n + 2 * t + half, 256, stride=16), :] = res[:, t * 128 : (t + 1) * 128]

        loop(0, 4, columns)

    def out_weight_rows(i):
        out_weight_part(gated, cot, owg_v, i, (c, prev, nxt, mine_o, far), True)

    done(l_cot)
    cot1 = row_first(cot)
    done(l_branch)
    branch1 = col_first(whole(branch))
    done(l_scan + l_gate)
    gate_forward()
    cot2 = row_second(cot, cot1)
    take_apart(0)
    branch2 = col_second(whole(branch), branch1)
    branch3 = col_third(whole(branch), branch2)
    arrived(*cot1[1:], *cot2)
    cot4 = cores(cot, 0)
    done(l_saved)
    saved1 = row_first(saved)
    done(l_ow)
    arrived(cot4)
    cot5 = cores(cot, 1)
    share(0)
    sa = sum0(0)
    arrived(cot5)
    share(1)
    sum1(0, sa)
    sb = sum0(1)
    take_apart(1)
    saved2 = row_second(saved, saved1)
    sum2(0, sa)
    sum3(0, sa)
    sum1(1, sb)
    sum2(1, sb)
    ga1 = sum4(0, sa)
    sum3(1, sb)
    take_apart(2)
    ga2 = col_second(batch(ggrad, 0), ga1)
    gb1 = sum4(1, sb)
    arrived(*saved1[1:], *saved2)
    saved4 = cores(saved, 0)
    take_apart(3)
    arrived(saved4)
    saved5 = cores(saved, 1)
    ga3 = col_third(batch(ggrad, 0), ga2)
    arrived(saved5)
    arrived(*branch2[2:], *branch3)
    in_weight_rows(0, 0)
    gb2 = col_second(batch(ggrad, 1), gb1)
    gated1 = col_first(whole(gated), (XP, XM))
    in_weight_rows(0, 1)
    arrived(*ga2[2:], *ga3)
    gb3 = col_third(batch(ggrad, 1), gb2)
    gated1 = col_first(whole(gated), (YH,)) + gated1
    input_share(0)
    ra = row0(0)
    in_weight_rows(0, 2)
    row1(0, ra)
    in_weight_rows(0, 3)
    row2(0, ra)
    arrived(*gb2[2:], *gb3)
    input_share(1)
    rb = row0(1)
    row3(0, ra)
    gated2 = col_second(whole(gated), gated1)
    row1(1, rb)
    in_weight_rows(1, 0)
    row2(1, rb)
    in_weight_rows(1, 1)
    row3(1, rb)
    in_weight_rows(1, 2)
    row4(0, ra)
    in_weight_rows(1, 3)
    gated3 = col_third_x(whole(gated), gated2)
    row4(1, rb)
    arrived(*gated2[:2])
    for i in range(4):
        out_weight_rows(i)
    arrived(*gated3)
    for copy in sent:
        copy.wait_send()


def write_out(ig, sg, iwg, owg, cot, gated, ig_out, sg_out, iwg_out, owg_out, sem):
    def store(i, src, dst):
        copy = pltpu.make_async_copy(src, dst, sem.at[i])
        copy.start()
        return copy

    copies = [store(0, iwg, iwg_out), store(1, sg, sg_out), store(2, ig, ig_out)]
    col = lax.axis_index("col")
    x, ho = col // 2, 1 - col % 2
    chunks = [(x + step) % 4 * 2 + ho for step in (1, 2, 3)]
    for i in range(4):
        out_weight_part(gated, cot, owg, i, chunks, False)
        rows = pl.ds(i * 256, 256)
        copies.append(store(3 + i, owg.at[rows], owg_out.at[rows]))
    for copy in copies:
        copy.wait()


def per_device(cot, saved, scan, gate, branch, ow, iw):
    iw = iw.reshape(1024, 2, 8, 128).transpose(0, 2, 1, 3).reshape(16384, 128)
    anywhere = pl.BlockSpec(memory_space=pl.ANY)
    tokens = pltpu.VMEM((2, 8, 128, 1024), BF16)

    def blocks(*shape):
        return pltpu.VMEM((*shape, 1024), BF16)

    results = ((128, 1024), BF16), ((256, 1024), BF16), ((16384, 128), F32), ((1024, 1024), F32)
    passed = (((2, 8, 128, 1024), BF16),) * 2
    held = pl.pallas_call(
        kernel,
        out_shape=[pltpu.VMEM(shape, dtype) for shape, dtype in results + passed],
        in_specs=[anywhere] * 7,
        out_specs=[pl.BlockSpec(memory_space=pltpu.VMEM)] * 6,
        scratch_shapes=[
            tokens,
            tokens,
            tokens,
            blocks(1024),
            blocks(2, 1024),
            pltpu.VMEM((2, 4096, 128), BF16),
            tokens,
            tokens,
            blocks(2, 128),
            blocks(2, 2, 64),
            blocks(2, 2, 128),
            blocks(2, 2, 128),
            blocks(2, 128),
            blocks(2, 8, 64),
            blocks(2, 64),
            blocks(2, 2, 64),
            blocks(2, 3, 64),
            blocks(2, 64),
            blocks(2, 128),
            blocks(2, 128),
            pltpu.SemaphoreType.DMA((REMOTE,)),
            pltpu.SemaphoreType.DMA((REMOTE,)),
            pltpu.SemaphoreType.DMA((LOCAL,)),
        ],
        compiler_params=pltpu.CompilerParams(
            collective_id=0, has_side_effects=True, vmem_limit_bytes=VMEM_LIMIT
        ),
        name="mixer_backward",
    )(cot, saved, scan, gate, branch, ow, iw)
    ig, sg, iwg, owg = pl.pallas_call(
        write_out,
        out_shape=[jax.ShapeDtypeStruct(shape, dtype) for shape, dtype in results],
        in_specs=[pl.BlockSpec(memory_space=pltpu.VMEM)] * 6,
        out_specs=[anywhere] * 4,
        scratch_shapes=[pltpu.SemaphoreType.DMA((7,))],
        compiler_params=pltpu.CompilerParams(vmem_limit_bytes=4 * 1024 * 1024),
        name="write_out",
    )(*[pltpu.with_memory_space_constraint(array, pltpu.VMEM) for array in held])
    iwg = iwg.reshape(1024, 8, 2, 128).transpose(0, 2, 1, 3).reshape(1024, 2, 1024)
    return ig, sg, iwg, owg


def solution(mesh):
    return jax.shard_map(
        per_device,
        mesh=mesh,
        in_specs=(
            P("row", "col"),
            P("row", "col"),
            P("col", "row"),
            P("col", "row"),
            P("col", "row"),
            P("row", "col"),
            P("col", None, "row"),
        ),
        out_specs=(P("row", "col"), P("col", "row"), P("col", None, "row"), P("row", "col")),
        check_vma=False,
    )
```

```python
import jax
import jax.numpy as jnp
from jax import lax
from jax.experimental import pallas as pl
from jax.experimental.pallas import tpu as pltpu
from jax.sharding import PartitionSpec as P

MESH = pl.DeviceIdType.MESH
F32 = jnp.float32
BF16 = jnp.bfloat16
REMOTE = 96
VMEM_LIMIT = 40 * 1024 * 1024
LOCAL = 24
NT = (((1,), (1,)), ((), ()))
NN = (((1,), (0,)), ((), ()))
TN = (((0,), (0,)), ((), ()))


def dot(a, b, dims):
    return lax.dot_general(a, b, dims, preferred_element_type=F32)


def loop(low, high, body):
    def step(i, carry):
        body(i)
        return carry

    lax.fori_loop(low, high, step, 0)


def tokens_of(buf, chunks, columns):
    return jnp.concatenate([buf[:, chunk, :, columns].reshape(256, columns.size) for chunk in chunks])


def out_weight_part(gated, cot, out, i, chunks, first):
    rows = pl.ds(i * 256, 256)
    res = dot(tokens_of(gated, chunks, rows), tokens_of(cot, chunks, pl.ds(0, 1024)), TN)
    out[rows] = res if first else out[rows] + res


def kernel(
    cot_in,
    saved_in,
    scan_in,
    gate_in,
    branch_in,
    ow_in,
    iw_in,
    ig_v,
    sg_v,
    iwg_v,
    owg_v,
    cot,
    gated,
    saved,
    branch,
    ggrad,
    ow,
    iw,
    iw_raw,
    part,
    part2,
    r_y0,
    r_half,
    r_q,
    r_x,
    r_y1,
    r2_core,
    r2_q,
    r2_x,
    r2_y,
    scan_v,
    gate_v,
    ssem,
    rsem,
    lsem,
):
    row, col = lax.axis_index("row"), lax.axis_index("col")
    yl, z, k = row // 8, (row // 2) % 4, row % 2
    x, h = col // 2, col % 2
    j = yl * 4 + z
    c = col

    def device(x=x, h=h, yl=yl, z=z, k=k):
        return ((yl * 4 + z) * 2 + k, x * 2 + h)

    xp, xm, x2 = (x + 1) % 4, (x + 3) % 4, (x + 2) % 4
    zp, zm, z2 = (z + 1) % 4, (z + 3) % 4, (z + 2) % 4
    ho, yo, ko = 1 - h, 1 - yl, 1 - k
    XP, XM, YH = device(x=xp), device(x=xm), device(h=ho)
    ZP, ZM, Z2, YL, CO = device(z=zp), device(z=zm), device(z=z2), device(yl=yo), device(k=ko)
    far_o, far, next_o, prev_o = x2 * 2 + ho, x2 * 2 + h, xp * 2 + ho, xm * 2 + ho
    nxt, prev, mine_o = xp * 2 + h, xm * 2 + h, x * 2 + ho

    used = [0, 0]
    sent = []

    def send(src, dst, to):
        i = used[0]
        used[0] += 1
        copy = pltpu.make_async_remote_copy(
            src_ref=src, dst_ref=dst, send_sem=ssem.at[i], recv_sem=rsem.at[i], device_id=to, device_id_type=MESH
        )
        copy.start()
        sent.append(copy)
        return copy

    def local(src, dst):
        i = used[1]
        used[1] += 1
        copy = pltpu.make_async_copy(src, dst, lsem.at[i])
        copy.start()
        return copy

    def arrived(*copies):
        for copy in copies:
            copy.wait_recv()

    def done(copies):
        for copy in copies:
            copy.wait()

    def row_block(src, buf):
        return [local(src.at[pl.ds(b * 64, 64)], buf.at[b, j, pl.ds(k * 64, 64)]) for b in range(2)]

    def col_block(src, dst):
        return [
            local(src.at[pl.ds(core * 128 + b * 64, 64)], dst(b).at[pl.ds(core * 64, 64)])
            for core in range(2)
            for b in range(2)
        ]

    l_cot = row_block(cot_in, cot)
    l_branch = col_block(branch_in, lambda b: branch.at[b, c])
    l_scan = col_block(scan_in, lambda b: scan_v.at[b])
    l_gate = col_block(gate_in, lambda b: gate_v.at[b])
    l_saved = row_block(saved_in, saved)
    l_iw = [local(iw_in.at[pl.ds(p * 4096, 4096)], iw_raw.at[p]) for p in range(2)]
    l_ow = [local(ow_in, ow)]

    barrier = pltpu.get_barrier_semaphore()
    for peer in (XP, XM, YH, ZP, ZM, Z2, YL, CO):
        pl.semaphore_signal(barrier, inc=1, device_id=peer, device_id_type=MESH)
    pl.semaphore_wait(barrier, 8)

    def mine_of(buf, chip, b):
        return buf.at[:, chip, pl.ds(k * 64, 64)] if b is None else buf.at[b, chip, pl.ds(k * 64, 64)]

    def row_first(buf, b=None):
        own = mine_of(buf, j, b)
        return [send(own, own, to) for to in (YL, Z2, ZP, ZM)]

    def row_second(buf, first, b=None):
        arrived(first[0])
        other = mine_of(buf, yo * 4 + z, b)
        return [send(other, other, to) for to in ((ZP, ZM, Z2) if b is None else (ZP, ZM))]

    def row_third(buf, first, b):
        arrived(first[1])
        far_z = mine_of(buf, yl * 4 + z2, b)
        return send(far_z, far_z, YL)

    def cores(buf, b):
        block = buf.at[b, :, pl.ds(k * 64, 64)]
        return send(block, block, CO)

    def col_first(at, to=(YH, XP, XM)):
        return [send(at(c), at(c), peer) for peer in to]

    def col_halves(at, first):
        arrived(first[1])
        a = send(at(prev, 0), at(prev, 0), XP)
        arrived(first[2])
        return [a, send(at(nxt, 1), at(nxt, 1), XM)]

    def col_other(at, first):
        arrived(first[0])
        return [send(at(mine_o), at(mine_o), to) for to in (XP, XM)]

    def col_second(at, first):
        return col_halves(at, first) + col_other(at, first)

    def col_first_split(at):
        ways = ((0, XP), (1, XM), (1, XP), (0, XM))
        return [send(at(c, half), at(c, half), peer) for half, peer in ways]

    def col_third(at, second, halves=(0, 1)):
        out = []
        for half in halves:
            arrived(second[half])
            out.append(send(at(far, half), at(far, half), YH))
        return out

    def whole(buf):
        def at(chunk, half=None):
            return buf.at[:, chunk] if half is None else buf.at[half, chunk]

        return at

    def batch(buf, b):
        def at(chunk, half=None):
            return buf.at[b, chunk] if half is None else buf.at[b, chunk, pl.ds(half * 64, 64)]

        return at

    to_row = lax.broadcasted_iota(jnp.int32, (256, 256), 0)
    from_row = lax.broadcasted_iota(jnp.int32, (256, 256), 1)
    permutation = ((to_row % 16) * 16 + to_row // 16 == from_row).astype(BF16)

    def take_apart(p):
        slot = p % 2
        l_iw[p].wait()

        def block(i):
            raw = iw_raw[slot, pl.ds(pl.multiple_of(i * 256, 256), 256)]
            apart = dot(permutation, raw, NN).astype(BF16)
            rows = pl.ds(pl.multiple_of(p * 256 + i * 16, 16), 16)
            for g in range(16):
                iw[g % 2, rows, (g // 2) * 128 : (g // 2 + 1) * 128] = apart[g * 16 : (g + 1) * 16]

        loop(0, 16, block)
        if p < 2:
            l_iw.append(local(iw_in.at[pl.ds((p + 2) * 4096, 4096)], iw_raw.at[slot]))

    def add_to(dst, *srcs):
        def rows_of(i):
            rows = pl.ds(pl.multiple_of(i * 16, 16), 16)
            total = dst[rows].astype(F32)
            for src in srcs:
                total = total + src[rows].astype(F32)
            dst[rows] = total.astype(BF16)

        loop(0, dst.shape[0] // 16, rows_of)

    def gate_forward():
        def rows_of(i):
            b, rows = i // 8, pl.ds(pl.multiple_of((i % 8) * 16, 16), 16)
            v = gate_v[b, rows].astype(F32)
            gated[b, c, rows] = (scan_v[b, rows].astype(F32) * (v * jax.nn.sigmoid(v))).astype(BF16)

        loop(0, 16, rows_of)

    def share(b):
        rows = cot[b].reshape(1024, 1024)

        def columns(n):
            at = pl.ds(pl.multiple_of(n * 256, 256), 256)
            part[b, :, :, at] = dot(rows, ow[at], NT).astype(BF16).reshape(8, 128, 256)

        loop(0, 4, columns)

    LOW, HIGH = pl.ds(0, 64), pl.ds(64, 64)

    def sum0(b):
        return dict(
            d=send(part.at[b, far_o], r_y0.at[b], YH),
            q=[send(part.at[b, next_o], r_q.at[b, 0], XP), send(part.at[b, prev_o], r_q.at[b, 1], XM)],
            e=[
                send(part.at[b, nxt, HIGH], r_x.at[b, 0, HIGH], XP),
                send(part.at[b, prev, LOW], r_x.at[b, 1, LOW], XM),
            ],
        )

    def sum1(b, s):
        arrived(s["d"])
        add_to(part.at[b, far], r_y0.at[b])
        s["f"] = [
            send(part.at[b, far, LOW], r_half.at[b, 0], XP),
            send(part.at[b, far, HIGH], r_half.at[b, 1], XM),
        ]

    def sum2(b, s):
        arrived(*s["q"])
        add_to(part.at[b, mine_o], r_q.at[b, 0], r_q.at[b, 1])
        s["y"] = send(part.at[b, mine_o], r_y1.at[b], YH)

    def sum3(b, s):
        arrived(s["f"][0])
        add_to(part.at[b, nxt, LOW], r_half.at[b, 0])
        g0 = send(part.at[b, nxt, LOW], r_x.at[b, 0, LOW], XP)
        arrived(s["f"][1])
        add_to(part.at[b, prev, HIGH], r_half.at[b, 1])
        g1 = send(part.at[b, prev, HIGH], r_x.at[b, 1, HIGH], XM)
        s["g"] = [g0, g1]

    def sum4(b, s):
        arrived(*s["e"], s["y"], *s["g"])

        def rows_of(i):
            rows = pl.ds(pl.multiple_of(i * 16, 16), 16)
            total = part[b, c, rows].astype(F32) + r_x[b, 0, rows].astype(F32)
            total = total + r_x[b, 1, rows].astype(F32) + r_y1[b, rows].astype(F32)
            v = gate_v[b, rows].astype(F32)
            s = jax.nn.sigmoid(v)
            ggrad[b, c, rows] = (total * scan_v[b, rows].astype(F32) * s * (1.0 + v * (1.0 - s))).astype(BF16)
            sg_v[pl.ds(pl.multiple_of((i // 4) * 128 + b * 64 + (i % 4) * 16, 16), 16)] = (total * (v * s)).astype(BF16)

        loop(0, 8, rows_of)
        return col_first(batch(ggrad, b))

    def input_share(b):
        def columns(n):
            at = pl.ds(pl.multiple_of(n * 256, 256), 256)
            total = dot(branch[b].reshape(1024, 1024), iw[0, at], NT)
            total = total + dot(ggrad[b].reshape(1024, 1024), iw[1, at], NT)
            part2[b, :, :, at] = total.astype(BF16).reshape(8, 128, 256)

        loop(0, 4, columns)

    MINE = pl.ds(pl.multiple_of(k * 64, 64), 64)
    OTHER = pl.ds(pl.multiple_of(ko * 64, 64), 64)

    def row0(b):
        return dict(c=send(part2.at[b, :, OTHER], r2_core.at[b], CO))

    def row1(b, s):
        arrived(s["c"])

        def chip(i):
            total = part2[b, i, MINE].astype(F32) + r2_core[b, i].astype(F32)
            part2[b, i, MINE] = total.astype(BF16)

        loop(0, 8, chip)
        ways = ((zp, ZP), (zm, ZM), (z2, Z2))
        s["q"] = [send(part2.at[b, yo * 4 + to, MINE], r2_q.at[b, i], dev) for i, (to, dev) in enumerate(ways)]
        s["x"] = [send(part2.at[b, yl * 4 + to, MINE], r2_x.at[b, i], dev) for i, (to, dev) in enumerate(ways)]

    def row3(b, s):
        arrived(*s["q"])
        add_to(part2.at[b, yo * 4 + z, MINE], r2_q.at[b, 0], r2_q.at[b, 1], r2_q.at[b, 2])
        s["y"] = send(part2.at[b, yo * 4 + z, MINE], r2_y.at[b], YL)

    def row4(b, s):
        arrived(*s["x"], s["y"])

        def rows_of(i):
            rows = pl.ds(pl.multiple_of(i * 16, 16), 16)
            own = pl.ds(pl.multiple_of(k * 64 + i * 16, 16), 16)
            total = part2[b, j, own].astype(F32) + r2_y[b, rows].astype(F32)
            for t in range(3):
                total = total + r2_x[b, t, rows].astype(F32)
            ig_v[pl.ds(pl.multiple_of(b * 64 + i * 16, 16), 16)] = total.astype(BF16)

        loop(0, 4, rows_of)

    def in_weight_rows(half, i):
        buf = (branch, ggrad)[half]
        lhs = saved[:, :, :, i * 256 : (i + 1) * 256].reshape(2048, 256)

        res = dot(lhs, buf[...].reshape(2048, 1024), TN)
        for t in range(8):
            iwg_v[pl.ds(i * 4096 + 2 * t + half, 256, stride=16), :] = res[:, t * 128 : (t + 1) * 128]

    def out_weight_rows(i):
        out_weight_part(gated, cot, owg_v, i, (c, prev, nxt, mine_o, far), True)

    done(l_cot)
    cot1 = row_first(cot)
    done(l_branch)
    branch1 = col_first(whole(branch))
    done(l_scan + l_gate)
    gate_forward()
    cot2 = row_second(cot, cot1)
    take_apart(0)
    branch2 = col_second(whole(branch), branch1)
    done(l_saved)
    saved1 = row_first(saved)
    branch3 = col_third(whole(branch), branch2, (0,))
    arrived(*cot1[1:], *cot2)
    cot4 = cores(cot, 0)
    done(l_ow)
    arrived(cot4)
    cot5 = cores(cot, 1)
    share(0)
    sa = sum0(0)
    arrived(cot5)
    share(1)
    sum1(0, sa)
    sb = sum0(1)
    take_apart(1)
    saved2 = row_second(saved, saved1)
    sum2(0, sa)
    sum3(0, sa)
    sum1(1, sb)
    sum2(1, sb)
    ga1 = sum4(0, sa)
    branch3 += col_third(whole(branch), branch2, (1,))
    sum3(1, sb)
    take_apart(2)
    ga2 = col_second(batch(ggrad, 0), ga1)
    gb1 = sum4(1, sb)
    arrived(*saved1[1:], *saved2)
    saved4 = cores(saved, 0)
    take_apart(3)
    ga3 = col_third(batch(ggrad, 0), ga2)
    arrived(saved4)
    saved5 = cores(saved, 1)
    arrived(*branch2[2:], *branch3)
    arrived(saved5)
    in_weight_rows(0, 0)
    in_weight_rows(0, 1)
    gb2 = col_second(batch(ggrad, 1), gb1)
    gated1 = col_first_split(whole(gated))
    in_weight_rows(0, 2)
    gb3 = col_third(batch(ggrad, 1), gb2)
    gated1 = col_first(whole(gated), (YH,)) + gated1
    arrived(*ga2[2:], *ga3)
    input_share(0)
    ra = row0(0)
    in_weight_rows(0, 3)
    row1(0, ra)
    arrived(*gb2[2:], *gb3)
    input_share(1)
    rb = row0(1)
    gated2 = col_halves(whole(gated), gated1)
    row3(0, ra)
    in_weight_rows(1, 0)
    gated2 += col_other(whole(gated), gated1)
    row1(1, rb)
    in_weight_rows(1, 1)
    gated3 = col_third(whole(gated), gated2, (0,))
    in_weight_rows(1, 2)
    row4(0, ra)
    in_weight_rows(1, 3)
    row3(1, rb)
    gated3 += col_third(whole(gated), gated2, (1,))
    arrived(*gated1[3:])
    for i in range(4):
        out_weight_rows(i)
    row4(1, rb)
    arrived(*gated2[2:], *gated3)
    for copy in sent:
        copy.wait_send()


def write_out(ig, sg, iwg, owg, cot, gated, ig_out, sg_out, iwg_out, owg_out, sem):
    def store(i, src, dst):
        copy = pltpu.make_async_copy(src, dst, sem.at[i])
        copy.start()
        return copy

    copies = [store(0, iwg, iwg_out), store(1, sg, sg_out), store(2, ig, ig_out)]
    col = lax.axis_index("col")
    x, ho = col // 2, 1 - col % 2
    chunks = [(x + step) % 4 * 2 + ho for step in (1, 2, 3)]
    for i in range(4):
        out_weight_part(gated, cot, owg, i, chunks, False)
        rows = pl.ds(i * 256, 256)
        copies.append(store(3 + i, owg.at[rows], owg_out.at[rows]))
    for copy in copies:
        copy.wait()


def per_device(cot, saved, scan, gate, branch, ow, iw):
    iw = iw.reshape(1024, 2, 8, 128).transpose(0, 2, 1, 3).reshape(16384, 128)
    anywhere = pl.BlockSpec(memory_space=pl.ANY)
    tokens = pltpu.VMEM((2, 8, 128, 1024), BF16)

    def blocks(*shape):
        return pltpu.VMEM((*shape, 1024), BF16)

    results = ((128, 1024), BF16), ((256, 1024), BF16), ((16384, 128), F32), ((1024, 1024), F32)
    passed = (((2, 8, 128, 1024), BF16),) * 2
    held = pl.pallas_call(
        kernel,
        out_shape=[pltpu.VMEM(shape, dtype) for shape, dtype in results + passed],
        in_specs=[anywhere] * 7,
        out_specs=[pl.BlockSpec(memory_space=pltpu.VMEM)] * 6,
        scratch_shapes=[
            tokens,
            tokens,
            tokens,
            blocks(1024),
            blocks(2, 1024),
            pltpu.VMEM((2, 4096, 128), BF16),
            tokens,
            tokens,
            blocks(2, 128),
            blocks(2, 2, 64),
            blocks(2, 2, 128),
            blocks(2, 2, 128),
            blocks(2, 128),
            blocks(2, 8, 64),
            blocks(2, 3, 64),
            blocks(2, 3, 64),
            blocks(2, 64),
            blocks(2, 128),
            blocks(2, 128),
            pltpu.SemaphoreType.DMA((REMOTE,)),
            pltpu.SemaphoreType.DMA((REMOTE,)),
            pltpu.SemaphoreType.DMA((LOCAL,)),
        ],
        compiler_params=pltpu.CompilerParams(
            collective_id=0, has_side_effects=True, vmem_limit_bytes=VMEM_LIMIT
        ),
        name="mixer_backward",
    )(cot, saved, scan, gate, branch, ow, iw)
    ig, sg, iwg, owg = pl.pallas_call(
        write_out,
        out_shape=[jax.ShapeDtypeStruct(shape, dtype) for shape, dtype in results],
        in_specs=[pl.BlockSpec(memory_space=pltpu.VMEM)] * 6,
        out_specs=[anywhere] * 4,
        scratch_shapes=[pltpu.SemaphoreType.DMA((7,))],
        compiler_params=pltpu.CompilerParams(vmem_limit_bytes=4 * 1024 * 1024),
        name="write_out",
    )(*[pltpu.with_memory_space_constraint(array, pltpu.VMEM) for array in held])
    iwg = iwg.reshape(1024, 8, 2, 128).transpose(0, 2, 1, 3).reshape(1024, 2, 1024)
    return ig, sg, iwg, owg


def solution(mesh):
    return jax.shard_map(
        per_device,
        mesh=mesh,
        in_specs=(
            P("row", "col"),
            P("row", "col"),
            P("col", "row"),
            P("col", "row"),
            P("col", "row"),
            P("row", "col"),
            P("col", None, "row"),
        ),
        out_specs=(P("row", "col"), P("col", "row"), P("col", None, "row"), P("row", "col")),
        check_vma=False,
    )
```

```python
import jax
import jax.numpy as jnp
from jax import lax
from jax.experimental import pallas as pl
from jax.experimental.pallas import tpu as pltpu
from jax.sharding import PartitionSpec as P

MESH = pl.DeviceIdType.MESH
F32 = jnp.float32
BF16 = jnp.bfloat16
REMOTE = 96
VMEM_LIMIT = 40 * 1024 * 1024
LOCAL = 24
NT = (((1,), (1,)), ((), ()))
NN = (((1,), (0,)), ((), ()))
TN = (((0,), (0,)), ((), ()))


def dot(a, b, dims):
    return lax.dot_general(a, b, dims, preferred_element_type=F32)


def loop(low, high, body):
    def step(i, carry):
        body(i)
        return carry

    lax.fori_loop(low, high, step, 0)


def tokens_of(buf, chunks, columns):
    return jnp.concatenate([buf[:, chunk, :, columns].reshape(256, columns.size) for chunk in chunks])


def out_weight_part(gated, cot, out, i, chunks, first):
    rows = pl.ds(i * 256, 256)
    res = dot(tokens_of(gated, chunks, rows), tokens_of(cot, chunks, pl.ds(0, 1024)), TN)
    out[rows] = res if first else out[rows] + res


def kernel(
    cot_in,
    saved_in,
    scan_in,
    gate_in,
    branch_in,
    ow_in,
    iw_in,
    ig_v,
    sg_v,
    iwg_v,
    owg_v,
    cot,
    gated,
    saved,
    branch,
    ggrad,
    ow,
    iw,
    iw_raw,
    part,
    part2,
    r_y0,
    r_half,
    r_q,
    r_x,
    r_y1,
    r2_core,
    r2_q,
    r2_x,
    r2_y,
    scan_v,
    gate_v,
    ssem,
    rsem,
    lsem,
):
    row, col = lax.axis_index("row"), lax.axis_index("col")
    yl, z, k = row // 8, (row // 2) % 4, row % 2
    x, h = col // 2, col % 2
    j = yl * 4 + z
    c = col

    def device(x=x, h=h, yl=yl, z=z, k=k):
        return ((yl * 4 + z) * 2 + k, x * 2 + h)

    xp, xm, x2 = (x + 1) % 4, (x + 3) % 4, (x + 2) % 4
    zp, zm, z2 = (z + 1) % 4, (z + 3) % 4, (z + 2) % 4
    ho, yo, ko = 1 - h, 1 - yl, 1 - k
    XP, XM, YH = device(x=xp), device(x=xm), device(h=ho)
    ZP, ZM, Z2, YL, CO = device(z=zp), device(z=zm), device(z=z2), device(yl=yo), device(k=ko)
    far_o, far, next_o, prev_o = x2 * 2 + ho, x2 * 2 + h, xp * 2 + ho, xm * 2 + ho
    nxt, prev, mine_o = xp * 2 + h, xm * 2 + h, x * 2 + ho

    used = [0, 0]
    sent = []

    def send(src, dst, to):
        i = used[0]
        used[0] += 1
        copy = pltpu.make_async_remote_copy(
            src_ref=src, dst_ref=dst, send_sem=ssem.at[i], recv_sem=rsem.at[i], device_id=to, device_id_type=MESH
        )
        copy.start()
        sent.append(copy)
        return copy

    def local(src, dst):
        i = used[1]
        used[1] += 1
        copy = pltpu.make_async_copy(src, dst, lsem.at[i])
        copy.start()
        return copy

    def arrived(*copies):
        for copy in copies:
            copy.wait_recv()

    def done(copies):
        for copy in copies:
            copy.wait()

    def row_block(src, buf):
        return [local(src.at[pl.ds(b * 64, 64)], buf.at[b, j, pl.ds(k * 64, 64)]) for b in range(2)]

    def col_block(src, dst):
        return [
            local(src.at[pl.ds(core * 128 + b * 64, 64)], dst(b).at[pl.ds(core * 64, 64)])
            for core in range(2)
            for b in range(2)
        ]

    l_cot = row_block(cot_in, cot)
    l_branch = col_block(branch_in, lambda b: branch.at[b, c])
    l_scan = col_block(scan_in, lambda b: scan_v.at[b])
    l_gate = col_block(gate_in, lambda b: gate_v.at[b])
    l_saved = row_block(saved_in, saved)
    l_iw = [local(iw_in.at[pl.ds(p * 4096, 4096)], iw_raw.at[p]) for p in range(2)]
    l_ow = [local(ow_in, ow)]

    barrier = pltpu.get_barrier_semaphore()
    for peer in (XP, XM, YH, ZP, ZM, Z2, YL, CO):
        pl.semaphore_signal(barrier, inc=1, device_id=peer, device_id_type=MESH)
    pl.semaphore_wait(barrier, 8)

    def mine_of(buf, chip, b):
        return buf.at[:, chip, pl.ds(k * 64, 64)] if b is None else buf.at[b, chip, pl.ds(k * 64, 64)]

    def row_first(buf, b=None):
        own = mine_of(buf, j, b)
        return [send(own, own, to) for to in (YL, Z2, ZP, ZM)]

    def row_second(buf, first, b=None):
        arrived(first[0])
        other = mine_of(buf, yo * 4 + z, b)
        return [send(other, other, to) for to in ((ZP, ZM, Z2) if b is None else (ZP, ZM))]

    def row_third(buf, first, b):
        arrived(first[1])
        far_z = mine_of(buf, yl * 4 + z2, b)
        return send(far_z, far_z, YL)

    def cores(buf, b):
        block = buf.at[b, :, pl.ds(k * 64, 64)]
        return send(block, block, CO)

    def col_first(at, to=(YH, XP, XM)):
        return [send(at(c), at(c), peer) for peer in to]

    def col_halves(at, first):
        arrived(first[1])
        a = send(at(prev, 0), at(prev, 0), XP)
        arrived(first[2])
        return [a, send(at(nxt, 1), at(nxt, 1), XM)]

    def col_other(at, first):
        arrived(first[0])
        return [send(at(mine_o), at(mine_o), to) for to in (XP, XM)]

    def col_second(at, first):
        return col_halves(at, first) + col_other(at, first)

    def col_first_split(at, ways):
        return [send(at(c, half), at(c, half), peer) for half, peer in ways]

    def col_third(at, second, halves=(0, 1)):
        out = []
        for half in halves:
            arrived(second[half])
            out.append(send(at(far, half), at(far, half), YH))
        return out

    def whole(buf):
        def at(chunk, half=None):
            return buf.at[:, chunk] if half is None else buf.at[half, chunk]

        return at

    def batch(buf, b):
        def at(chunk, half=None):
            return buf.at[b, chunk] if half is None else buf.at[b, chunk, pl.ds(half * 64, 64)]

        return at

    to_row = lax.broadcasted_iota(jnp.int32, (256, 256), 0)
    from_row = lax.broadcasted_iota(jnp.int32, (256, 256), 1)
    permutation = ((to_row % 16) * 16 + to_row // 16 == from_row).astype(BF16)

    def take_apart(p):
        slot = p % 2
        l_iw[p].wait()

        def block(i):
            raw = iw_raw[slot, pl.ds(pl.multiple_of(i * 256, 256), 256)]
            apart = dot(permutation, raw, NN).astype(BF16)
            rows = pl.ds(pl.multiple_of(p * 256 + i * 16, 16), 16)
            for g in range(16):
                iw[g % 2, rows, (g // 2) * 128 : (g // 2 + 1) * 128] = apart[g * 16 : (g + 1) * 16]

        loop(0, 16, block)
        if p < 2:
            l_iw.append(local(iw_in.at[pl.ds((p + 2) * 4096, 4096)], iw_raw.at[slot]))

    def add_to(dst, *srcs):
        def rows_of(i):
            rows = pl.ds(pl.multiple_of(i * 16, 16), 16)
            total = dst[rows].astype(F32)
            for src in srcs:
                total = total + src[rows].astype(F32)
            dst[rows] = total.astype(BF16)

        loop(0, dst.shape[0] // 16, rows_of)

    def gate_forward():
        def rows_of(i):
            b, rows = i // 8, pl.ds(pl.multiple_of((i % 8) * 16, 16), 16)
            v = gate_v[b, rows].astype(F32)
            gated[b, c, rows] = (scan_v[b, rows].astype(F32) * (v * jax.nn.sigmoid(v))).astype(BF16)

        loop(0, 16, rows_of)

    def share(b):
        rows = cot[b].reshape(1024, 1024)

        def columns(n):
            at = pl.ds(pl.multiple_of(n * 256, 256), 256)
            part[b, :, :, at] = dot(rows, ow[at], NT).astype(BF16).reshape(8, 128, 256)

        loop(0, 4, columns)

    LOW, HIGH = pl.ds(0, 64), pl.ds(64, 64)

    def sum0(b):
        return dict(
            d=send(part.at[b, far_o], r_y0.at[b], YH),
            q=[send(part.at[b, next_o], r_q.at[b, 0], XP), send(part.at[b, prev_o], r_q.at[b, 1], XM)],
            e=[
                send(part.at[b, nxt, HIGH], r_x.at[b, 0, HIGH], XP),
                send(part.at[b, prev, LOW], r_x.at[b, 1, LOW], XM),
            ],
        )

    def sum1(b, s):
        arrived(s["d"])
        add_to(part.at[b, far], r_y0.at[b])
        s["f"] = [
            send(part.at[b, far, LOW], r_half.at[b, 0], XP),
            send(part.at[b, far, HIGH], r_half.at[b, 1], XM),
        ]

    def sum2(b, s):
        arrived(*s["q"])
        add_to(part.at[b, mine_o], r_q.at[b, 0], r_q.at[b, 1])
        s["y"] = send(part.at[b, mine_o], r_y1.at[b], YH)

    def sum3(b, s):
        arrived(s["f"][0])
        add_to(part.at[b, nxt, LOW], r_half.at[b, 0])
        g0 = send(part.at[b, nxt, LOW], r_x.at[b, 0, LOW], XP)
        arrived(s["f"][1])
        add_to(part.at[b, prev, HIGH], r_half.at[b, 1])
        g1 = send(part.at[b, prev, HIGH], r_x.at[b, 1, HIGH], XM)
        s["g"] = [g0, g1]

    def sum4(b, s):
        arrived(*s["e"], s["y"], *s["g"])

        def rows_of(i):
            rows = pl.ds(pl.multiple_of(i * 16, 16), 16)
            total = part[b, c, rows].astype(F32) + r_x[b, 0, rows].astype(F32)
            total = total + r_x[b, 1, rows].astype(F32) + r_y1[b, rows].astype(F32)
            v = gate_v[b, rows].astype(F32)
            s = jax.nn.sigmoid(v)
            ggrad[b, c, rows] = (total * scan_v[b, rows].astype(F32) * s * (1.0 + v * (1.0 - s))).astype(BF16)
            sg_v[pl.ds(pl.multiple_of((i // 4) * 128 + b * 64 + (i % 4) * 16, 16), 16)] = (total * (v * s)).astype(BF16)

        loop(0, 8, rows_of)
        return col_first(batch(ggrad, b))

    def input_share(b):
        def columns(n):
            at = pl.ds(pl.multiple_of(n * 256, 256), 256)
            total = dot(branch[b].reshape(1024, 1024), iw[0, at], NT)
            total = total + dot(ggrad[b].reshape(1024, 1024), iw[1, at], NT)
            part2[b, :, :, at] = total.astype(BF16).reshape(8, 128, 256)

        loop(0, 4, columns)

    def input_share_branch(b):
        def columns(n):
            at = pl.ds(pl.multiple_of(n * 256, 256), 256)
            owg_v[:, at] = dot(branch[b].reshape(1024, 1024), iw[0, at], NT)

        loop(0, 4, columns)

    def input_share_gate(b, low, high):
        def columns(n):
            at = pl.ds(pl.multiple_of(n * 256, 256), 256)
            total = owg_v[:, at] + dot(ggrad[b].reshape(1024, 1024), iw[1, at], NT)
            part2[b, :, :, at] = total.astype(BF16).reshape(8, 128, 256)

        loop(low, high, columns)

    MINE = pl.ds(pl.multiple_of(k * 64, 64), 64)
    OTHER = pl.ds(pl.multiple_of(ko * 64, 64), 64)

    def row0(b):
        return dict(c=send(part2.at[b, :, OTHER], r2_core.at[b], CO))

    def row1(b, s):
        arrived(s["c"])

        def chip(i):
            total = part2[b, i, MINE].astype(F32) + r2_core[b, i].astype(F32)
            part2[b, i, MINE] = total.astype(BF16)

        loop(0, 8, chip)
        ways = ((zp, ZP), (zm, ZM), (z2, Z2))
        s["q"] = [send(part2.at[b, yo * 4 + to, MINE], r2_q.at[b, i], dev) for i, (to, dev) in enumerate(ways)]
        s["x"] = [send(part2.at[b, yl * 4 + to, MINE], r2_x.at[b, i], dev) for i, (to, dev) in enumerate(ways)]

    def row3(b, s):
        arrived(*s["q"])
        add_to(part2.at[b, yo * 4 + z, MINE], r2_q.at[b, 0], r2_q.at[b, 1], r2_q.at[b, 2])
        s["y"] = send(part2.at[b, yo * 4 + z, MINE], r2_y.at[b], YL)

    def row4(b, s):
        arrived(*s["x"], s["y"])

        def rows_of(i):
            rows = pl.ds(pl.multiple_of(i * 16, 16), 16)
            own = pl.ds(pl.multiple_of(k * 64 + i * 16, 16), 16)
            total = part2[b, j, own].astype(F32) + r2_y[b, rows].astype(F32)
            for t in range(3):
                total = total + r2_x[b, t, rows].astype(F32)
            ig_v[pl.ds(pl.multiple_of(b * 64 + i * 16, 16), 16)] = total.astype(BF16)

        loop(0, 4, rows_of)

    def in_weight_rows(half, i):
        buf = (branch, ggrad)[half]
        lhs = saved[:, :, :, i * 256 : (i + 1) * 256].reshape(2048, 256)

        res = dot(lhs, buf[...].reshape(2048, 1024), TN)
        for t in range(8):
            iwg_v[pl.ds(i * 4096 + 2 * t + half, 256, stride=16), :] = res[:, t * 128 : (t + 1) * 128]

    def out_weight_rows(i):
        out_weight_part(gated, cot, owg_v, i, (c, prev, nxt, mine_o, far), True)

    done(l_cot)
    cot1 = row_first(cot)
    done(l_branch)
    branch1 = col_first(whole(branch))
    done(l_scan + l_gate)
    gate_forward()
    cot2 = row_second(cot, cot1)
    take_apart(0)
    branch2 = col_second(whole(branch), branch1)
    done(l_saved)
    saved1 = row_first(saved)
    branch3 = col_third(whole(branch), branch2, (0,))
    arrived(*cot1[1:], *cot2)
    cot4 = cores(cot, 0)
    done(l_ow)
    arrived(cot4)
    cot5 = cores(cot, 1)
    share(0)
    sa = sum0(0)
    arrived(cot5)
    share(1)
    sum1(0, sa)
    sb = sum0(1)
    take_apart(1)
    saved2 = row_second(saved, saved1)
    sum2(0, sa)
    sum3(0, sa)
    sum1(1, sb)
    sum2(1, sb)
    ga1 = sum4(0, sa)
    branch3 += col_third(whole(branch), branch2, (1,))
    sum3(1, sb)
    take_apart(2)
    ga2 = col_second(batch(ggrad, 0), ga1)
    gb1 = sum4(1, sb)
    gated1 = col_first_split(whole(gated), ((0, XP), (1, XM)))
    arrived(*saved1[1:], *saved2)
    saved4 = cores(saved, 0)
    take_apart(3)
    ga3 = col_third(batch(ggrad, 0), ga2)
    gated1 = col_first(whole(gated), (YH,)) + gated1
    arrived(saved4)
    saved5 = cores(saved, 1)
    arrived(*branch2[2:], *branch3)
    input_share_branch(1)
    arrived(saved5)
    in_weight_rows(0, 0)
    in_weight_rows(0, 1)
    gb2 = col_second(batch(ggrad, 1), gb1)
    in_weight_rows(0, 2)
    in_weight_rows(0, 3)
    arrived(*ga2[2:], *ga3)
    input_share(0)
    ra = row0(0)
    gated2 = col_halves(whole(gated), gated1)
    gated1 += col_first_split(whole(gated), ((1, XP), (0, XM)))
    gb3 = col_third(batch(ggrad, 1), gb2)
    row1(0, ra)
    gated2 += col_other(whole(gated), gated1)
    arrived(*gb2[2:], *gb3)
    input_share_gate(1, 0, 3)
    gated3 = col_third(whole(gated), gated2, (0,))
    input_share_gate(1, 3, 4)
    rb = row0(1)
    row3(0, ra)
    in_weight_rows(1, 0)
    gated3 += col_third(whole(gated), gated2, (1,))
    row1(1, rb)
    in_weight_rows(1, 1)
    in_weight_rows(1, 2)
    in_weight_rows(1, 3)
    row4(0, ra)
    row3(1, rb)
    arrived(*gated1[3:])
    for i in range(4):
        out_weight_rows(i)
    row4(1, rb)
    arrived(*gated2[2:], *gated3)
    for copy in sent:
        copy.wait_send()


def write_out(ig, sg, iwg, owg, cot, gated, ig_out, sg_out, iwg_out, owg_out, sem):
    def store(i, src, dst):
        copy = pltpu.make_async_copy(src, dst, sem.at[i])
        copy.start()
        return copy

    copies = [store(0, iwg, iwg_out), store(1, sg, sg_out), store(2, ig, ig_out)]
    col = lax.axis_index("col")
    x, ho = col // 2, 1 - col % 2
    chunks = [(x + step) % 4 * 2 + ho for step in (1, 2, 3)]
    for i in range(4):
        out_weight_part(gated, cot, owg, i, chunks, False)
        rows = pl.ds(i * 256, 256)
        copies.append(store(3 + i, owg.at[rows], owg_out.at[rows]))
    for copy in copies:
        copy.wait()


def per_device(cot, saved, scan, gate, branch, ow, iw):
    iw = iw.reshape(1024, 2, 8, 128).transpose(0, 2, 1, 3).reshape(16384, 128)
    anywhere = pl.BlockSpec(memory_space=pl.ANY)
    tokens = pltpu.VMEM((2, 8, 128, 1024), BF16)

    def blocks(*shape):
        return pltpu.VMEM((*shape, 1024), BF16)

    results = ((128, 1024), BF16), ((256, 1024), BF16), ((16384, 128), F32), ((1024, 1024), F32)
    passed = (((2, 8, 128, 1024), BF16),) * 2
    held = pl.pallas_call(
        kernel,
        out_shape=[pltpu.VMEM(shape, dtype) for shape, dtype in results + passed],
        in_specs=[anywhere] * 7,
        out_specs=[pl.BlockSpec(memory_space=pltpu.VMEM)] * 6,
        scratch_shapes=[
            tokens,
            tokens,
            tokens,
            blocks(1024),
            blocks(2, 1024),
            pltpu.VMEM((2, 4096, 128), BF16),
            tokens,
            tokens,
            blocks(2, 128),
            blocks(2, 2, 64),
            blocks(2, 2, 128),
            blocks(2, 2, 128),
            blocks(2, 128),
            blocks(2, 8, 64),
            blocks(2, 3, 64),
            blocks(2, 3, 64),
            blocks(2, 64),
            blocks(2, 128),
            blocks(2, 128),
            pltpu.SemaphoreType.DMA((REMOTE,)),
            pltpu.SemaphoreType.DMA((REMOTE,)),
            pltpu.SemaphoreType.DMA((LOCAL,)),
        ],
        compiler_params=pltpu.CompilerParams(
            collective_id=0, has_side_effects=True, vmem_limit_bytes=VMEM_LIMIT
        ),
        name="mixer_backward",
    )(cot, saved, scan, gate, branch, ow, iw)
    ig, sg, iwg, owg = pl.pallas_call(
        write_out,
        out_shape=[jax.ShapeDtypeStruct(shape, dtype) for shape, dtype in results],
        in_specs=[pl.BlockSpec(memory_space=pltpu.VMEM)] * 6,
        out_specs=[anywhere] * 4,
        scratch_shapes=[pltpu.SemaphoreType.DMA((7,))],
        compiler_params=pltpu.CompilerParams(vmem_limit_bytes=4 * 1024 * 1024),
        name="write_out",
    )(*[pltpu.with_memory_space_constraint(array, pltpu.VMEM) for array in held])
    iwg = iwg.reshape(1024, 8, 2, 128).transpose(0, 2, 1, 3).reshape(1024, 2, 1024)
    return ig, sg, iwg, owg


def solution(mesh):
    return jax.shard_map(
        per_device,
        mesh=mesh,
        in_specs=(
            P("row", "col"),
            P("row", "col"),
            P("col", "row"),
            P("col", "row"),
            P("col", "row"),
            P("row", "col"),
            P("col", None, "row"),
        ),
        out_specs=(P("row", "col"), P("col", "row"), P("col", None, "row"), P("row", "col")),
        check_vma=False,
    )
```

```python
import jax
import jax.numpy as jnp
from jax import lax
from jax.experimental import pallas as pl
from jax.experimental.pallas import tpu as pltpu
from jax.sharding import PartitionSpec as P

MESH = pl.DeviceIdType.MESH
F32 = jnp.float32
BF16 = jnp.bfloat16
REMOTE = 96
VMEM_LIMIT = 40 * 1024 * 1024
LOCAL = 24
NT = (((1,), (1,)), ((), ()))
NN = (((1,), (0,)), ((), ()))
TN = (((0,), (0,)), ((), ()))


def dot(a, b, dims):
    return lax.dot_general(a, b, dims, preferred_element_type=F32)


def loop(low, high, body):
    def step(i, carry):
        body(i)
        return carry

    lax.fori_loop(low, high, step, 0)


def tokens_of(buf, chunks, columns):
    return jnp.concatenate([buf[:, chunk, :, columns].reshape(256, columns.size) for chunk in chunks])


def out_weight_part(gated, cot, out, i, chunks, first):
    rows = pl.ds(i * 256, 256)
    res = dot(tokens_of(gated, chunks, rows), tokens_of(cot, chunks, pl.ds(0, 1024)), TN)
    out[rows] = res if first else out[rows] + res


def kernel(
    cot_in,
    saved_in,
    scan_in,
    gate_in,
    branch_in,
    ow_in,
    iw_in,
    ig_v,
    sg_v,
    iwg_v,
    owg_v,
    cot,
    gated,
    saved,
    branch,
    ggrad,
    ow,
    iw,
    iw_raw,
    part,
    part2,
    r_y0,
    r_half,
    r_q,
    r_x,
    r_y1,
    r2_core,
    r2_q,
    r2_x,
    r2_y,
    scan_v,
    gate_v,
    ssem,
    rsem,
    lsem,
):
    row, col = lax.axis_index("row"), lax.axis_index("col")
    yl, z, k = row // 8, (row // 2) % 4, row % 2
    x, h = col // 2, col % 2
    j = yl * 4 + z
    c = col

    def device(x=x, h=h, yl=yl, z=z, k=k):
        return ((yl * 4 + z) * 2 + k, x * 2 + h)

    xp, xm, x2 = (x + 1) % 4, (x + 3) % 4, (x + 2) % 4
    zp, zm, z2 = (z + 1) % 4, (z + 3) % 4, (z + 2) % 4
    ho, yo, ko = 1 - h, 1 - yl, 1 - k
    XP, XM, YH = device(x=xp), device(x=xm), device(h=ho)
    ZP, ZM, Z2, YL, CO = device(z=zp), device(z=zm), device(z=z2), device(yl=yo), device(k=ko)
    far_o, far, next_o, prev_o = x2 * 2 + ho, x2 * 2 + h, xp * 2 + ho, xm * 2 + ho
    nxt, prev, mine_o = xp * 2 + h, xm * 2 + h, x * 2 + ho

    used = [0, 0]
    sent = []

    def send(src, dst, to):
        i = used[0]
        used[0] += 1
        copy = pltpu.make_async_remote_copy(
            src_ref=src, dst_ref=dst, send_sem=ssem.at[i], recv_sem=rsem.at[i], device_id=to, device_id_type=MESH
        )
        copy.start()
        sent.append(copy)
        return copy

    def local(src, dst):
        i = used[1]
        used[1] += 1
        copy = pltpu.make_async_copy(src, dst, lsem.at[i])
        copy.start()
        return copy

    def arrived(*copies):
        for copy in copies:
            copy.wait_recv()

    def done(copies):
        for copy in copies:
            copy.wait()

    def row_block(src, buf):
        return [local(src.at[pl.ds(b * 64, 64)], buf.at[b, j, pl.ds(k * 64, 64)]) for b in range(2)]

    def col_block(src, dst):
        return [
            local(src.at[pl.ds(core * 128 + b * 64, 64)], dst(b).at[pl.ds(core * 64, 64)])
            for core in range(2)
            for b in range(2)
        ]

    l_cot = row_block(cot_in, cot)
    l_branch = col_block(branch_in, lambda b: branch.at[b, c])
    l_scan = col_block(scan_in, lambda b: scan_v.at[b])
    l_gate = col_block(gate_in, lambda b: gate_v.at[b])
    l_saved = row_block(saved_in, saved)
    l_iw = [local(iw_in.at[pl.ds(p * 4096, 4096)], iw_raw.at[p]) for p in range(2)]
    l_ow = [local(ow_in, ow)]

    barrier = pltpu.get_barrier_semaphore()
    for peer in (XP, XM, YH, ZP, ZM, Z2, YL, CO):
        pl.semaphore_signal(barrier, inc=1, device_id=peer, device_id_type=MESH)
    pl.semaphore_wait(barrier, 8)

    def mine_of(buf, chip, b):
        return buf.at[:, chip, pl.ds(k * 64, 64)] if b is None else buf.at[b, chip, pl.ds(k * 64, 64)]

    def row_first(buf, b=None):
        own = mine_of(buf, j, b)
        return [send(own, own, to) for to in (YL, Z2, ZP, ZM)]

    def row_second(buf, first, b=None):
        arrived(first[0])
        other = mine_of(buf, yo * 4 + z, b)
        return [send(other, other, to) for to in ((ZP, ZM, Z2) if b is None else (ZP, ZM))]

    def row_third(buf, first, b):
        arrived(first[1])
        far_z = mine_of(buf, yl * 4 + z2, b)
        return send(far_z, far_z, YL)

    def cores(buf, b):
        block = buf.at[b, :, pl.ds(k * 64, 64)]
        return send(block, block, CO)

    def col_first(at, to=(YH, XP, XM)):
        return [send(at(c), at(c), peer) for peer in to]

    def col_halves(at, first):
        arrived(first[1])
        a = send(at(prev, 0), at(prev, 0), XP)
        arrived(first[2])
        return [a, send(at(nxt, 1), at(nxt, 1), XM)]

    def col_other(at, first):
        arrived(first[0])
        return [send(at(mine_o), at(mine_o), to) for to in (XP, XM)]

    def col_second(at, first):
        return col_halves(at, first) + col_other(at, first)

    def col_first_split(at, ways):
        return [send(at(c, half), at(c, half), peer) for half, peer in ways]

    def col_third(at, second, halves=(0, 1)):
        out = []
        for half in halves:
            arrived(second[half])
            out.append(send(at(far, half), at(far, half), YH))
        return out

    def whole(buf):
        def at(chunk, half=None):
            return buf.at[:, chunk] if half is None else buf.at[half, chunk]

        return at

    def batch(buf, b):
        def at(chunk, half=None):
            return buf.at[b, chunk] if half is None else buf.at[b, chunk, pl.ds(half * 64, 64)]

        return at

    to_row = lax.broadcasted_iota(jnp.int32, (256, 256), 0)
    from_row = lax.broadcasted_iota(jnp.int32, (256, 256), 1)
    permutation = ((to_row % 16) * 16 + to_row // 16 == from_row).astype(BF16)

    def take_apart(p):
        slot = p % 2
        l_iw[p].wait()

        def block(i):
            raw = iw_raw[slot, pl.ds(pl.multiple_of(i * 256, 256), 256)]
            apart = dot(permutation, raw, NN).astype(BF16)
            rows = pl.ds(pl.multiple_of(p * 256 + i * 16, 16), 16)
            for g in range(16):
                iw[g % 2, rows, (g // 2) * 128 : (g // 2 + 1) * 128] = apart[g * 16 : (g + 1) * 16]

        loop(0, 16, block)
        if p < 2:
            l_iw.append(local(iw_in.at[pl.ds((p + 2) * 4096, 4096)], iw_raw.at[slot]))

    def add_to(dst, *srcs):
        def rows_of(i):
            rows = pl.ds(pl.multiple_of(i * 16, 16), 16)
            total = dst[rows].astype(F32)
            for src in srcs:
                total = total + src[rows].astype(F32)
            dst[rows] = total.astype(BF16)

        loop(0, dst.shape[0] // 16, rows_of)

    def gate_forward():
        def rows_of(i):
            b, rows = i // 8, pl.ds(pl.multiple_of((i % 8) * 16, 16), 16)
            v = gate_v[b, rows].astype(F32)
            gated[b, c, rows] = (scan_v[b, rows].astype(F32) * (v * jax.nn.sigmoid(v))).astype(BF16)

        loop(0, 16, rows_of)

    def share(b):
        rows = cot[b].reshape(1024, 1024)

        def columns(n):
            at = pl.ds(pl.multiple_of(n * 256, 256), 256)
            part[b, :, :, at] = dot(rows, ow[at], NT).astype(BF16).reshape(8, 128, 256)

        loop(0, 4, columns)

    LOW, HIGH = pl.ds(0, 64), pl.ds(64, 64)

    def sum0(b):
        return dict(
            d=send(part.at[b, far_o], r_y0.at[b], YH),
            q=[send(part.at[b, next_o], r_q.at[b, 0], XP), send(part.at[b, prev_o], r_q.at[b, 1], XM)],
            e=[
                send(part.at[b, nxt, HIGH], r_x.at[b, 0, HIGH], XP),
                send(part.at[b, prev, LOW], r_x.at[b, 1, LOW], XM),
            ],
        )

    def sum1(b, s):
        arrived(s["d"])
        add_to(part.at[b, far], r_y0.at[b])
        s["f"] = [
            send(part.at[b, far, LOW], r_half.at[b, 0], XP),
            send(part.at[b, far, HIGH], r_half.at[b, 1], XM),
        ]

    def sum2(b, s):
        arrived(*s["q"])
        add_to(part.at[b, mine_o], r_q.at[b, 0], r_q.at[b, 1])
        s["y"] = send(part.at[b, mine_o], r_y1.at[b], YH)

    def sum3(b, s):
        arrived(s["f"][0])
        add_to(part.at[b, nxt, LOW], r_half.at[b, 0])
        g0 = send(part.at[b, nxt, LOW], r_x.at[b, 0, LOW], XP)
        arrived(s["f"][1])
        add_to(part.at[b, prev, HIGH], r_half.at[b, 1])
        g1 = send(part.at[b, prev, HIGH], r_x.at[b, 1, HIGH], XM)
        s["g"] = [g0, g1]

    def sum4(b, s):
        arrived(*s["e"], s["y"], *s["g"])

        def rows_of(i):
            rows = pl.ds(pl.multiple_of(i * 16, 16), 16)
            total = part[b, c, rows].astype(F32) + r_x[b, 0, rows].astype(F32)
            total = total + r_x[b, 1, rows].astype(F32) + r_y1[b, rows].astype(F32)
            v = gate_v[b, rows].astype(F32)
            s = jax.nn.sigmoid(v)
            ggrad[b, c, rows] = (total * scan_v[b, rows].astype(F32) * s * (1.0 + v * (1.0 - s))).astype(BF16)
            sg_v[pl.ds(pl.multiple_of((i // 4) * 128 + b * 64 + (i % 4) * 16, 16), 16)] = (total * (v * s)).astype(BF16)

        loop(0, 8, rows_of)
        return col_first(batch(ggrad, b))

    def input_share(b):
        def columns(n):
            at = pl.ds(pl.multiple_of(n * 256, 256), 256)
            total = dot(branch[b].reshape(1024, 1024), iw[0, at], NT)
            total = total + dot(ggrad[b].reshape(1024, 1024), iw[1, at], NT)
            part2[b, :, :, at] = total.astype(BF16).reshape(8, 128, 256)

        loop(0, 4, columns)

    MINE = pl.ds(pl.multiple_of(k * 64, 64), 64)
    OTHER = pl.ds(pl.multiple_of(ko * 64, 64), 64)
    HALVES = ((OTHER, pl.ds(0, 512)), (MINE, pl.ds(512, 512)))

    def input_share_branch(b):
        for tokens, rows in HALVES:

            def columns(n):
                at = pl.ds(pl.multiple_of(n * 256, 256), 256)
                owg_v[rows, at] = dot(branch[b, :, tokens].reshape(512, 1024), iw[0, at], NT)

            loop(0, 4, columns)

    def input_share_gate(b, half, low=0, high=4):
        tokens, rows = HALVES[half]

        def columns(n):
            at = pl.ds(pl.multiple_of(n * 256, 256), 256)
            total = owg_v[rows, at] + dot(ggrad[b, :, tokens].reshape(512, 1024), iw[1, at], NT)
            part2[b, :, tokens, at] = total.astype(BF16).reshape(8, 64, 256)

        loop(low, high, columns)

    def row0(b):
        return dict(c=send(part2.at[b, :, OTHER], r2_core.at[b], CO))

    def row1(b, s):
        arrived(s["c"])

        def chip(i):
            total = part2[b, i, MINE].astype(F32) + r2_core[b, i].astype(F32)
            part2[b, i, MINE] = total.astype(BF16)

        loop(0, 8, chip)
        ways = ((z2, Z2), (zp, ZP), (zm, ZM))
        s["q"] = [send(part2.at[b, yo * 4 + to, MINE], r2_q.at[b, i], dev) for i, (to, dev) in enumerate(ways)]
        s["x"] = [send(part2.at[b, yl * 4 + to, MINE], r2_x.at[b, i], dev) for i, (to, dev) in enumerate(ways)]

    def row3(b, s):
        arrived(*s["q"])
        add_to(part2.at[b, yo * 4 + z, MINE], r2_q.at[b, 0], r2_q.at[b, 1], r2_q.at[b, 2])
        s["y"] = send(part2.at[b, yo * 4 + z, MINE], r2_y.at[b], YL)

    def row4(b, s):
        arrived(*s["x"], s["y"])

        def rows_of(i):
            rows = pl.ds(pl.multiple_of(i * 16, 16), 16)
            own = pl.ds(pl.multiple_of(k * 64 + i * 16, 16), 16)
            total = part2[b, j, own].astype(F32) + r2_y[b, rows].astype(F32)
            for t in range(3):
                total = total + r2_x[b, t, rows].astype(F32)
            ig_v[pl.ds(pl.multiple_of(b * 64 + i * 16, 16), 16)] = total.astype(BF16)

        loop(0, 4, rows_of)

    def in_weight_rows(half, i):
        buf = (branch, ggrad)[half]
        lhs = saved[:, :, :, i * 256 : (i + 1) * 256].reshape(2048, 256)

        res = dot(lhs, buf[...].reshape(2048, 1024), TN)
        for t in range(8):
            iwg_v[pl.ds(i * 4096 + 2 * t + half, 256, stride=16), :] = res[:, t * 128 : (t + 1) * 128]

    def out_weight_rows(i):
        out_weight_part(gated, cot, owg_v, i, (c, prev, nxt, mine_o, far), True)

    done(l_cot)
    cot1 = row_first(cot)
    done(l_branch)
    branch1 = col_first(whole(branch))
    done(l_scan + l_gate)
    gate_forward()
    cot2 = row_second(cot, cot1)
    take_apart(0)
    branch2 = col_second(whole(branch), branch1)
    done(l_saved)
    saved1 = row_first(saved)
    branch3 = col_third(whole(branch), branch2, (0,))
    arrived(*cot1[1:], *cot2)
    cot4 = cores(cot, 0)
    done(l_ow)
    arrived(cot4)
    cot5 = cores(cot, 1)
    share(0)
    sa = sum0(0)
    arrived(cot5)
    share(1)
    sum1(0, sa)
    sb = sum0(1)
    take_apart(1)
    saved2 = row_second(saved, saved1)
    sum2(0, sa)
    sum3(0, sa)
    sum1(1, sb)
    sum2(1, sb)
    ga1 = sum4(0, sa)
    branch3 += col_third(whole(branch), branch2, (1,))
    sum3(1, sb)
    take_apart(2)
    ga2 = col_second(batch(ggrad, 0), ga1)
    gb1 = sum4(1, sb)
    gated1 = col_first_split(whole(gated), ((0, XP), (1, XM)))
    arrived(*saved1[1:], *saved2)
    saved4 = cores(saved, 0)
    take_apart(3)
    ga3 = col_third(batch(ggrad, 0), ga2)
    gated1 = col_first(whole(gated), (YH,)) + gated1
    arrived(saved4)
    saved5 = cores(saved, 1)
    arrived(*branch2[2:], *branch3)
    input_share_branch(1)
    arrived(saved5)
    in_weight_rows(0, 0)
    in_weight_rows(0, 1)
    gb2 = col_second(batch(ggrad, 1), gb1)
    arrived(*ga2[2:], *ga3)
    input_share(0)
    ra = row0(0)
    gated2 = col_halves(whole(gated), gated1)
    gated1 += col_first_split(whole(gated), ((1, XP), (0, XM)))
    gb3 = col_third(batch(ggrad, 1), gb2)
    row1(0, ra)
    in_weight_rows(0, 2)
    gated2 += col_other(whole(gated), gated1)
    in_weight_rows(0, 3)
    arrived(*gb2[2:], *gb3)
    input_share_gate(1, 0)
    rb = row0(1)
    row3(0, ra)
    input_share_gate(1, 1, 0, 2)
    gated3 = col_third(whole(gated), gated2, (0,))
    input_share_gate(1, 1, 2, 4)
    row1(1, rb)
    gated3 += col_third(whole(gated), gated2, (1,))
    for i in range(4):
        in_weight_rows(1, i)
    row4(0, ra)
    row3(1, rb)
    arrived(*gated1[3:])
    for i in range(4):
        out_weight_rows(i)
    row4(1, rb)
    arrived(*gated2[2:], *gated3)
    for copy in sent:
        copy.wait_send()


def write_out(ig, sg, iwg, owg, cot, gated, ig_out, sg_out, iwg_out, owg_out, sem):
    def store(i, src, dst):
        copy = pltpu.make_async_copy(src, dst, sem.at[i])
        copy.start()
        return copy

    quarters = [pl.ds(i * 4096, 4096) for i in range(4)]
    copies = [store(6 + i, iwg.at[rows], iwg_out.at[rows]) for i, rows in enumerate(quarters)]
    copies += [store(0, sg, sg_out), store(1, ig, ig_out)]
    col = lax.axis_index("col")
    x, ho = col // 2, 1 - col % 2
    chunks = [(x + step) % 4 * 2 + ho for step in (1, 2, 3)]
    for i in range(4):
        out_weight_part(gated, cot, owg, i, chunks, False)
        rows = pl.ds(i * 256, 256)
        copies.append(store(2 + i, owg.at[rows], owg_out.at[rows]))
    for copy in copies:
        copy.wait()


def per_device(cot, saved, scan, gate, branch, ow, iw):
    iw = iw.reshape(1024, 2, 8, 128).transpose(0, 2, 1, 3).reshape(16384, 128)
    anywhere = pl.BlockSpec(memory_space=pl.ANY)
    tokens = pltpu.VMEM((2, 8, 128, 1024), BF16)

    def blocks(*shape):
        return pltpu.VMEM((*shape, 1024), BF16)

    results = ((128, 1024), BF16), ((256, 1024), BF16), ((16384, 128), F32), ((1024, 1024), F32)
    passed = (((2, 8, 128, 1024), BF16),) * 2
    held = pl.pallas_call(
        kernel,
        out_shape=[pltpu.VMEM(shape, dtype) for shape, dtype in results + passed],
        in_specs=[anywhere] * 7,
        out_specs=[pl.BlockSpec(memory_space=pltpu.VMEM)] * 6,
        scratch_shapes=[
            tokens,
            tokens,
            tokens,
            blocks(1024),
            blocks(2, 1024),
            pltpu.VMEM((2, 4096, 128), BF16),
            tokens,
            tokens,
            blocks(2, 128),
            blocks(2, 2, 64),
            blocks(2, 2, 128),
            blocks(2, 2, 128),
            blocks(2, 128),
            blocks(2, 8, 64),
            blocks(2, 3, 64),
            blocks(2, 3, 64),
            blocks(2, 64),
            blocks(2, 128),
            blocks(2, 128),
            pltpu.SemaphoreType.DMA((REMOTE,)),
            pltpu.SemaphoreType.DMA((REMOTE,)),
            pltpu.SemaphoreType.DMA((LOCAL,)),
        ],
        compiler_params=pltpu.CompilerParams(
            collective_id=0, has_side_effects=True, vmem_limit_bytes=VMEM_LIMIT
        ),
        name="mixer_backward",
    )(cot, saved, scan, gate, branch, ow, iw)
    ig, sg, iwg, owg = pl.pallas_call(
        write_out,
        out_shape=[jax.ShapeDtypeStruct(shape, dtype) for shape, dtype in results],
        in_specs=[pl.BlockSpec(memory_space=pltpu.VMEM)] * 6,
        out_specs=[anywhere] * 4,
        scratch_shapes=[pltpu.SemaphoreType.DMA((10,))],
        compiler_params=pltpu.CompilerParams(vmem_limit_bytes=4 * 1024 * 1024),
        name="write_out",
    )(*[pltpu.with_memory_space_constraint(array, pltpu.VMEM) for array in held])
    iwg = iwg.reshape(1024, 8, 2, 128).transpose(0, 2, 1, 3).reshape(1024, 2, 1024)
    return ig, sg, iwg, owg


def solution(mesh):
    return jax.shard_map(
        per_device,
        mesh=mesh,
        in_specs=(
            P("row", "col"),
            P("row", "col"),
            P("col", "row"),
            P("col", "row"),
            P("col", "row"),
            P("row", "col"),
            P("col", None, "row"),
        ),
        out_specs=(P("row", "col"), P("col", "row"), P("col", None, "row"), P("row", "col")),
        check_vma=False,
    )
```

```python
import jax
import jax.numpy as jnp
from jax import lax
from jax.experimental import pallas as pl
from jax.experimental.pallas import tpu as pltpu
from jax.sharding import PartitionSpec as P

MESH = pl.DeviceIdType.MESH
F32 = jnp.float32
BF16 = jnp.bfloat16
REMOTE = 96
VMEM_LIMIT = 40 * 1024 * 1024
LOCAL = 24
NT = (((1,), (1,)), ((), ()))
NN = (((1,), (0,)), ((), ()))
TN = (((0,), (0,)), ((), ()))


def dot(a, b, dims):
    return lax.dot_general(a, b, dims, preferred_element_type=F32)


def loop(low, high, body):
    def step(i, carry):
        body(i)
        return carry

    lax.fori_loop(low, high, step, 0)


def tokens_of(buf, chunks, columns):
    return jnp.concatenate([buf[:, chunk, :, columns].reshape(256, columns.size) for chunk in chunks])


def out_weight_part(gated, cot, out, i, chunks, first):
    rows = pl.ds(i * 256, 256)
    res = dot(tokens_of(gated, chunks, rows), tokens_of(cot, chunks, pl.ds(0, 1024)), TN)
    out[rows] = res if first else out[rows] + res


def kernel(
    cot_in,
    saved_in,
    scan_in,
    gate_in,
    branch_in,
    ow_in,
    iw_in,
    ig_v,
    sg_v,
    iwg_v,
    owg_v,
    cot,
    gated,
    saved,
    branch,
    ggrad,
    ow,
    iw,
    iw_raw,
    part,
    part2,
    r_y0,
    r_half,
    r_q,
    r_x,
    r_y1,
    r2_core,
    r2_q,
    r2_x,
    r2_y,
    scan_v,
    gate_v,
    ssem,
    rsem,
    lsem,
):
    row, col = lax.axis_index("row"), lax.axis_index("col")
    yl, z, k = row // 8, (row // 2) % 4, row % 2
    x, h = col // 2, col % 2
    j = yl * 4 + z
    c = col

    def device(x=x, h=h, yl=yl, z=z, k=k):
        return ((yl * 4 + z) * 2 + k, x * 2 + h)

    xp, xm, x2 = (x + 1) % 4, (x + 3) % 4, (x + 2) % 4
    zp, zm, z2 = (z + 1) % 4, (z + 3) % 4, (z + 2) % 4
    ho, yo, ko = 1 - h, 1 - yl, 1 - k
    XP, XM, YH = device(x=xp), device(x=xm), device(h=ho)
    ZP, ZM, Z2, YL, CO = device(z=zp), device(z=zm), device(z=z2), device(yl=yo), device(k=ko)
    far_o, far, next_o, prev_o = x2 * 2 + ho, x2 * 2 + h, xp * 2 + ho, xm * 2 + ho
    nxt, prev, mine_o = xp * 2 + h, xm * 2 + h, x * 2 + ho

    used = [0, 0]
    sent = []

    def send(src, dst, to):
        i = used[0]
        used[0] += 1
        copy = pltpu.make_async_remote_copy(
            src_ref=src, dst_ref=dst, send_sem=ssem.at[i], recv_sem=rsem.at[i], device_id=to, device_id_type=MESH
        )
        copy.start()
        sent.append(copy)
        return copy

    def local(src, dst):
        i = used[1]
        used[1] += 1
        copy = pltpu.make_async_copy(src, dst, lsem.at[i])
        copy.start()
        return copy

    def arrived(*copies):
        for copy in copies:
            copy.wait_recv()

    def done(copies):
        for copy in copies:
            copy.wait()

    def row_block(src, buf):
        return [local(src.at[pl.ds(b * 64, 64)], buf.at[b, j, pl.ds(k * 64, 64)]) for b in range(2)]

    def col_block(src, dst):
        return [
            local(src.at[pl.ds(core * 128 + b * 64, 64)], dst(b).at[pl.ds(core * 64, 64)])
            for core in range(2)
            for b in range(2)
        ]

    l_cot = row_block(cot_in, cot)
    l_branch = col_block(branch_in, lambda b: branch.at[b, c])
    l_scan = col_block(scan_in, lambda b: scan_v.at[b])
    l_gate = col_block(gate_in, lambda b: gate_v.at[b])
    l_saved = row_block(saved_in, saved)
    l_iw = [local(iw_in.at[pl.ds(p * 4096, 4096)], iw_raw.at[p]) for p in range(2)]
    l_ow = [local(ow_in, ow)]

    barrier = pltpu.get_barrier_semaphore()
    for peer in (XP, XM, YH, ZP, ZM, Z2, YL, CO):
        pl.semaphore_signal(barrier, inc=1, device_id=peer, device_id_type=MESH)
    pl.semaphore_wait(barrier, 8)

    def mine_of(buf, chip, b):
        return buf.at[:, chip, pl.ds(k * 64, 64)] if b is None else buf.at[b, chip, pl.ds(k * 64, 64)]

    def row_first(buf, b=None):
        own = mine_of(buf, j, b)
        return [send(own, own, to) for to in (YL, Z2, ZP, ZM)]

    def row_second(buf, first, b=None):
        arrived(first[0])
        other = mine_of(buf, yo * 4 + z, b)
        return [send(other, other, to) for to in ((ZP, ZM, Z2) if b is None else (ZP, ZM))]

    def row_third(buf, first, b):
        arrived(first[1])
        far_z = mine_of(buf, yl * 4 + z2, b)
        return send(far_z, far_z, YL)

    def cores(buf, b):
        block = buf.at[b, :, pl.ds(k * 64, 64)]
        return send(block, block, CO)

    def col_first(at, to=(YH, XP, XM)):
        return [send(at(c), at(c), peer) for peer in to]

    def col_halves(at, first):
        arrived(first[1])
        a = send(at(prev, 0), at(prev, 0), XP)
        arrived(first[2])
        return [a, send(at(nxt, 1), at(nxt, 1), XM)]

    def col_other(at, first):
        arrived(first[0])
        return [send(at(mine_o), at(mine_o), to) for to in (XP, XM)]

    def col_second(at, first):
        return col_halves(at, first) + col_other(at, first)

    def col_first_split(at, ways):
        return [send(at(c, half), at(c, half), peer) for half, peer in ways]

    def col_third(at, second, halves=(0, 1)):
        out = []
        for half in halves:
            arrived(second[half])
            out.append(send(at(far, half), at(far, half), YH))
        return out

    def whole(buf):
        def at(chunk, half=None):
            return buf.at[:, chunk] if half is None else buf.at[half, chunk]

        return at

    def batch(buf, b):
        def at(chunk, half=None):
            return buf.at[b, chunk] if half is None else buf.at[b, chunk, pl.ds(half * 64, 64)]

        return at

    to_row = lax.broadcasted_iota(jnp.int32, (256, 256), 0)
    from_row = lax.broadcasted_iota(jnp.int32, (256, 256), 1)
    permutation = ((to_row % 16) * 16 + to_row // 16 == from_row).astype(BF16)

    def take_apart(p):
        slot = p % 2
        l_iw[p].wait()

        def block(i):
            raw = iw_raw[slot, pl.ds(pl.multiple_of(i * 256, 256), 256)]
            apart = dot(permutation, raw, NN).astype(BF16)
            rows = pl.ds(pl.multiple_of(p * 256 + i * 16, 16), 16)
            for g in range(16):
                iw[g % 2, rows, (g // 2) * 128 : (g // 2 + 1) * 128] = apart[g * 16 : (g + 1) * 16]

        loop(0, 16, block)
        if p < 2:
            l_iw.append(local(iw_in.at[pl.ds((p + 2) * 4096, 4096)], iw_raw.at[slot]))

    def add_to(dst, *srcs):
        def rows_of(i):
            rows = pl.ds(pl.multiple_of(i * 16, 16), 16)
            total = dst[rows].astype(F32)
            for src in srcs:
                total = total + src[rows].astype(F32)
            dst[rows] = total.astype(BF16)

        loop(0, dst.shape[0] // 16, rows_of)

    def gate_forward():
        def rows_of(i):
            b, rows = i // 8, pl.ds(pl.multiple_of((i % 8) * 16, 16), 16)
            v = gate_v[b, rows].astype(F32)
            gated[b, c, rows] = (scan_v[b, rows].astype(F32) * (v * jax.nn.sigmoid(v))).astype(BF16)

        loop(0, 16, rows_of)

    def share(b):
        rows = cot[b].reshape(1024, 1024)

        def columns(n):
            at = pl.ds(pl.multiple_of(n * 256, 256), 256)
            part[b, :, :, at] = dot(rows, ow[at], NT).astype(BF16).reshape(8, 128, 256)

        loop(0, 4, columns)

    LOW, HIGH = pl.ds(0, 64), pl.ds(64, 64)

    def sum0(b):
        return dict(
            d=send(part.at[b, far_o], r_y0.at[b], YH),
            q=[send(part.at[b, next_o], r_q.at[b, 0], XP), send(part.at[b, prev_o], r_q.at[b, 1], XM)],
            e=[
                send(part.at[b, nxt, HIGH], r_x.at[b, 0, HIGH], XP),
                send(part.at[b, prev, LOW], r_x.at[b, 1, LOW], XM),
            ],
        )

    def sum1(b, s):
        arrived(s["d"])
        add_to(part.at[b, far], r_y0.at[b])
        s["f"] = [
            send(part.at[b, far, LOW], r_half.at[b, 0], XP),
            send(part.at[b, far, HIGH], r_half.at[b, 1], XM),
        ]

    def sum2(b, s):
        arrived(*s["q"])
        add_to(part.at[b, mine_o], r_q.at[b, 0], r_q.at[b, 1])
        s["y"] = send(part.at[b, mine_o], r_y1.at[b], YH)

    def sum3(b, s):
        arrived(s["f"][0])
        add_to(part.at[b, nxt, LOW], r_half.at[b, 0])
        g0 = send(part.at[b, nxt, LOW], r_x.at[b, 0, LOW], XP)
        arrived(s["f"][1])
        add_to(part.at[b, prev, HIGH], r_half.at[b, 1])
        g1 = send(part.at[b, prev, HIGH], r_x.at[b, 1, HIGH], XM)
        s["g"] = [g0, g1]

    def sum4(b, s):
        arrived(*s["e"], s["y"], *s["g"])

        def rows_of(i):
            rows = pl.ds(pl.multiple_of(i * 16, 16), 16)
            total = part[b, c, rows].astype(F32) + r_x[b, 0, rows].astype(F32)
            total = total + r_x[b, 1, rows].astype(F32) + r_y1[b, rows].astype(F32)
            v = gate_v[b, rows].astype(F32)
            s = jax.nn.sigmoid(v)
            ggrad[b, c, rows] = (total * scan_v[b, rows].astype(F32) * s * (1.0 + v * (1.0 - s))).astype(BF16)
            sg_v[pl.ds(pl.multiple_of((i // 4) * 128 + b * 64 + (i % 4) * 16, 16), 16)] = (total * (v * s)).astype(BF16)

        loop(0, 8, rows_of)
        return col_first(batch(ggrad, b))

    def input_share(b):
        def columns(n):
            at = pl.ds(pl.multiple_of(n * 256, 256), 256)
            total = dot(branch[b].reshape(1024, 1024), iw[0, at], NT)
            total = total + dot(ggrad[b].reshape(1024, 1024), iw[1, at], NT)
            part2[b, :, :, at] = total.astype(BF16).reshape(8, 128, 256)

        loop(0, 4, columns)

    MINE = pl.ds(pl.multiple_of(k * 64, 64), 64)
    OTHER = pl.ds(pl.multiple_of(ko * 64, 64), 64)
    HALVES = ((OTHER, pl.ds(0, 512)), (MINE, pl.ds(512, 512)))

    def input_share_branch(b):
        for tokens, rows in HALVES:

            def columns(n):
                at = pl.ds(pl.multiple_of(n * 256, 256), 256)
                owg_v[rows, at] = dot(branch[b, :, tokens].reshape(512, 1024), iw[0, at], NT)

            loop(0, 4, columns)

    def input_share_gate(b, half, low=0, high=4):
        tokens, rows = HALVES[half]

        def columns(n):
            at = pl.ds(pl.multiple_of(n * 256, 256), 256)
            total = owg_v[rows, at] + dot(ggrad[b, :, tokens].reshape(512, 1024), iw[1, at], NT)
            part2[b, :, tokens, at] = total.astype(BF16).reshape(8, 64, 256)

        loop(low, high, columns)

    def row0(b):
        return dict(c=send(part2.at[b, :, OTHER], r2_core.at[b], CO))

    def row1(b, s):
        arrived(s["c"])

        def chip(i):
            total = part2[b, i, MINE].astype(F32) + r2_core[b, i].astype(F32)
            part2[b, i, MINE] = total.astype(BF16)

        loop(0, 8, chip)
        ways = ((z2, Z2), (zp, ZP), (zm, ZM))
        s["q"] = [send(part2.at[b, yo * 4 + to, MINE], r2_q.at[b, i], dev) for i, (to, dev) in enumerate(ways)]
        s["x"] = [send(part2.at[b, yl * 4 + to, MINE], r2_x.at[b, i], dev) for i, (to, dev) in enumerate(ways)]

    def row3(b, s):
        arrived(*s["q"])
        add_to(part2.at[b, yo * 4 + z, MINE], r2_q.at[b, 0], r2_q.at[b, 1], r2_q.at[b, 2])
        s["y"] = send(part2.at[b, yo * 4 + z, MINE], r2_y.at[b], YL)

    def row4(b, s):
        arrived(*s["x"], s["y"])

        def rows_of(i):
            rows = pl.ds(pl.multiple_of(i * 16, 16), 16)
            own = pl.ds(pl.multiple_of(k * 64 + i * 16, 16), 16)
            total = part2[b, j, own].astype(F32) + r2_y[b, rows].astype(F32)
            for t in range(3):
                total = total + r2_x[b, t, rows].astype(F32)
            ig_v[pl.ds(pl.multiple_of(b * 64 + i * 16, 16), 16)] = total.astype(BF16)

        loop(0, 4, rows_of)

    def in_weight_rows(half, i):
        buf = (branch, ggrad)[half]
        lhs = saved[:, :, :, i * 256 : (i + 1) * 256].reshape(2048, 256)

        res = dot(lhs, buf[...].reshape(2048, 1024), TN)
        for t in range(8):
            iwg_v[pl.ds(i * 4096 + 2 * t + half, 256, stride=16), :] = res[:, t * 128 : (t + 1) * 128]

    def out_weight_rows(i):
        out_weight_part(gated, cot, owg_v, i, (c, prev, nxt, mine_o, far), True)

    done(l_cot)
    cot1 = row_first(cot)
    done(l_branch)
    branch1 = col_first(whole(branch))
    done(l_scan + l_gate)
    gate_forward()
    cot2 = row_second(cot, cot1)
    take_apart(0)
    branch2 = col_second(whole(branch), branch1)
    done(l_saved)
    saved1 = row_first(saved)
    branch3 = col_third(whole(branch), branch2, (0,))
    arrived(*cot1[1:], *cot2)
    cot4 = cores(cot, 0)
    done(l_ow)
    arrived(cot4)
    cot5 = cores(cot, 1)
    share(0)
    sa = sum0(0)
    arrived(cot5)
    share(1)
    sum1(0, sa)
    sb = sum0(1)
    take_apart(1)
    saved2 = row_second(saved, saved1)
    sum2(0, sa)
    sum3(0, sa)
    sum1(1, sb)
    sum2(1, sb)
    ga1 = sum4(0, sa)
    branch3 += col_third(whole(branch), branch2, (1,))
    sum3(1, sb)
    take_apart(2)
    ga2 = col_second(batch(ggrad, 0), ga1)
    gb1 = sum4(1, sb)
    gated1 = col_first_split(whole(gated), ((0, XP), (1, XM)))
    arrived(*saved1[1:], *saved2)
    saved4 = cores(saved, 0)
    take_apart(3)
    ga3 = col_third(batch(ggrad, 0), ga2)
    gated1 = col_first(whole(gated), (YH,)) + gated1
    arrived(saved4)
    saved5 = cores(saved, 1)
    arrived(*branch2[2:], *branch3)
    input_share_branch(1)
    arrived(saved5)
    in_weight_rows(0, 0)
    in_weight_rows(0, 1)
    gb2 = col_second(batch(ggrad, 1), gb1)
    arrived(*ga2[2:], *ga3)
    input_share(0)
    ra = row0(0)
    gated2 = col_halves(whole(gated), gated1)
    gated1 += col_first_split(whole(gated), ((1, XP), (0, XM)))
    gb3 = col_third(batch(ggrad, 1), gb2)
    row1(0, ra)
    in_weight_rows(0, 2)
    gated2 += col_other(whole(gated), gated1)
    in_weight_rows(0, 3)
    arrived(*gb2[2:], *gb3)
    input_share_gate(1, 0)
    rb = row0(1)
    row3(0, ra)
    input_share_gate(1, 1, 0, 2)
    gated3 = col_third(whole(gated), gated2, (0,))
    input_share_gate(1, 1, 2, 4)
    row1(1, rb)
    gated3 += col_third(whole(gated), gated2, (1,))
    for i in range(4):
        in_weight_rows(1, i)
    row4(0, ra)
    row3(1, rb)
    arrived(*gated1[3:])
    for i in range(4):
        out_weight_rows(i)
    row4(1, rb)
    arrived(*gated2[2:], *gated3)
    for copy in sent:
        copy.wait_send()


def write_out(ig, sg, iwg, owg, cot, gated, ig_out, sg_out, iwg_out, owg_out, sem):
    def store(i, src, dst):
        copy = pltpu.make_async_copy(src, dst, sem.at[i])
        copy.start()
        return copy

    quarters = [pl.ds(i * 4096, 4096) for i in range(4)]
    copies = [store(6 + i, iwg.at[rows], iwg_out.at[rows]) for i, rows in enumerate(quarters)]
    copies += [store(0, sg, sg_out), store(1, ig, ig_out)]
    col = lax.axis_index("col")
    x, ho = col // 2, 1 - col % 2
    chunks = [(x + step) % 4 * 2 + ho for step in (1, 2, 3)]
    for i in range(4):
        out_weight_part(gated, cot, owg, i, chunks, False)
        rows = pl.ds(i * 256, 256)
        copies.append(store(2 + i, owg.at[rows], owg_out.at[rows]))
    for copy in copies:
        copy.wait()


def per_device(cot, saved, scan, gate, branch, ow, iw):
    iw = iw.reshape(1024, 2, 8, 128).transpose(0, 2, 1, 3).reshape(16384, 128)
    anywhere = pl.BlockSpec(memory_space=pl.ANY)
    tokens = pltpu.VMEM((2, 8, 128, 1024), BF16)

    def blocks(*shape):
        return pltpu.VMEM((*shape, 1024), BF16)

    results = ((128, 1024), BF16), ((256, 1024), BF16), ((16384, 128), F32), ((1024, 1024), F32)
    kept = results[:2] + (((16400, 128), F32),) + results[3:]
    passed = (((2, 8, 128, 1024), BF16),) * 2
    held = pl.pallas_call(
        kernel,
        out_shape=[pltpu.VMEM(shape, dtype) for shape, dtype in kept + passed],
        in_specs=[anywhere] * 7,
        out_specs=[pl.BlockSpec(memory_space=pltpu.VMEM)] * 6,
        scratch_shapes=[
            tokens,
            tokens,
            tokens,
            blocks(1024),
            blocks(2, 1024),
            pltpu.VMEM((2, 4096, 128), BF16),
            tokens,
            tokens,
            blocks(2, 128),
            blocks(2, 2, 64),
            blocks(2, 2, 128),
            blocks(2, 2, 128),
            blocks(2, 128),
            blocks(2, 8, 64),
            blocks(2, 3, 64),
            blocks(2, 3, 64),
            blocks(2, 64),
            blocks(2, 128),
            blocks(2, 128),
            pltpu.SemaphoreType.DMA((REMOTE,)),
            pltpu.SemaphoreType.DMA((REMOTE,)),
            pltpu.SemaphoreType.DMA((LOCAL,)),
        ],
        compiler_params=pltpu.CompilerParams(
            collective_id=0, has_side_effects=True, vmem_limit_bytes=VMEM_LIMIT
        ),
        name="mixer_backward",
    )(cot, saved, scan, gate, branch, ow, iw)
    ig, sg, iwg, owg = pl.pallas_call(
        write_out,
        out_shape=[jax.ShapeDtypeStruct(shape, dtype) for shape, dtype in results],
        in_specs=[pl.BlockSpec(memory_space=pltpu.VMEM)] * 6,
        out_specs=[anywhere] * 4,
        scratch_shapes=[pltpu.SemaphoreType.DMA((10,))],
        compiler_params=pltpu.CompilerParams(vmem_limit_bytes=4 * 1024 * 1024),
        name="write_out",
    )(*[pltpu.with_memory_space_constraint(array, pltpu.VMEM) for array in held])
    iwg = iwg.reshape(1024, 8, 2, 128).transpose(0, 2, 1, 3).reshape(1024, 2, 1024)
    return ig, sg, iwg, owg


def solution(mesh):
    return jax.shard_map(
        per_device,
        mesh=mesh,
        in_specs=(
            P("row", "col"),
            P("row", "col"),
            P("col", "row"),
            P("col", "row"),
            P("col", "row"),
            P("row", "col"),
            P("col", None, "row"),
        ),
        out_specs=(P("row", "col"), P("col", "row"), P("col", None, "row"), P("row", "col")),
        check_vma=False,
    )
```
